512 devices in a mesh: blk: 16 (over y_lo, x), grp: 32 (over y_hi, z, core).
Axes of the slice: x: 4, y: 8 (y_hi: 2, y_lo: 4; y = y_hi * 4 + y_lo), z: 8, core: 2. Of those that a mesh axis runs over, the one named last changes fastest.
Arguments:
- tower_images: bfloat16 [32768, 1152], P(('blk', 'grp')), may hold values from -0.17675781 to 0.17675781
- owners: int32 [32768], P(('blk', 'grp')), may hold values from 0 to 895, as said below
- counts: int32 [512], P(('blk', 'grp')), may hold values from 1 to 64, as said below
- text: bfloat16 [14336, 1152], P(('blk', 'grp')), may hold values from -0.17675781 to 0.17675781
- logit_scale: float32 [1], replicated, may hold values from 8 to 12
- logit_bias: float32 [1], replicated, may hold values from -6 to -3
Outputs:
- image_grad: float32 [32768, 1152], P(('blk', 'grp'))
- text_grad: float32 [14336, 1152], P(('blk', 'grp'))
The draws below stay inside these ranges and needn't reach their ends.
Inputs may be any that keep to these rules, and one draw needn't show every extreme that they name: `owners`: tower devices come in data groups of 32 consecutive devices. In each group the first counts[u] slots of tower u name pairs of that group, and every one of the group's 32 * 28 pairs is named by exactly one live slot; a pair index q belongs to owner device q // 28 of the group. At most 2 live slots of one tower name pairs of one owner, and some tower reaches 2 in every group. Slots past the count hold arbitrary indices in range. `counts`: live slots of a tower device; over a data group they sum to 896, and 64 is reached in every group.
All inputs are finite; a program needn't handle non-finite values.
Results may differ from the reference program's by a relative error of at most 0.005.
Values may be sent and summed in bfloat16 or wider, within the bound.
A program may use at most 64 MiB of HBM per device.

```python
import math
import jax
import jax.numpy as jnp
from jax import lax

D = 1152
PAIRS_DEV = 28
TOTAL = 14336
CAP = 64
N_BLK = 16
N_GRP = 32


def group_tables(key):
    heavy_count = N_GRP // 4
    light_count = N_GRP - heavy_count
    light_rows = PAIRS_DEV - N_GRP // 2
    first, second, third, fourth = jax.random.split(key, 4)
    relabel = jax.random.permutation(first, N_GRP).astype(jnp.int32)
    owner_dev = jnp.arange(N_GRP, dtype=jnp.int32)[:, None]
    row = jnp.arange(PAIRS_DEV, dtype=jnp.int32)[None, :]
    light = heavy_count + (owner_dev * light_rows + (row - N_GRP // 2)) % light_count
    heavy = row // 2
    base = jnp.where(row < N_GRP // 2, heavy, light)
    tower = relabel[base]
    scores = jax.random.randint(second, (N_GRP, PAIRS_DEV), 0, 1 << 20) * PAIRS_DEV + row
    local = jnp.argsort(scores, axis=1).astype(jnp.int32)
    owner = owner_dev * PAIRS_DEV + local
    tower_flat = tower.reshape(-1)
    owner_flat = owner.reshape(-1)
    shuffle = jax.random.permutation(third, N_GRP * PAIRS_DEV).astype(jnp.int32)
    order = jnp.argsort(tower_flat * (N_GRP * PAIRS_DEV) + shuffle).astype(jnp.int32)
    sorted_tower = tower_flat[order]
    sorted_owner = owner_flat[order]
    counts = jnp.sum((tower_flat[:, None] == jnp.arange(N_GRP, dtype=jnp.int32)[None, :]).astype(jnp.int32), axis=0)
    starts = jnp.cumsum(counts) - counts
    position = jnp.arange(N_GRP * PAIRS_DEV, dtype=jnp.int32) - starts[sorted_tower]
    filler = jax.random.randint(fourth, (N_GRP * CAP,), 0, N_GRP * PAIRS_DEV).astype(jnp.int32)
    table = filler.at[sorted_tower * CAP + position].set(sorted_owner)
    return (table, counts.astype(jnp.int32))


def route_tables(key):
    keys = jax.random.split(key, N_BLK)
    tables, counts = jax.vmap(group_tables)(keys)
    return (tables.reshape(-1), counts.reshape(-1))


def draw_owners(key, part):
    tables, counts = route_tables(key)
    return tables


def draw_counts(key, part):
    tables, counts = route_tables(key)
    return counts


def steps_of(stream_key, dims, cuts, smallest, high):
    def one(axis_at, shards_of):
        steps = jax.random.uniform(jax.random.fold_in(jax.random.fold_in(stream_key, 6), axis_at), (shards_of,), jnp.float32, smallest / len(cuts), high / len(cuts))
        return jnp.repeat(jnp.exp(steps), dims[axis_at] // shards_of).reshape((-1,) + (1,) * (len(dims) - axis_at - 1))

    level = one(*cuts[0])
    for cut in cuts[1:]:
        level = level * one(*cut)
    return level


def scatter_about(rng, shape, spread, bound, pieces=(), kind=jnp.bfloat16):
    drawn = jax.random.normal(rng, shape, jnp.float32) * spread
    if len(pieces) > 0:
        drawn = steps_of(rng, shape, pieces, -0.22, 0.18) * drawn
    return jnp.clip(drawn, min=-bound, max=bound).astype(kind)


def setup_inputs(seed: int = 0) -> dict:
    arg_keys = jax.random.split(jax.random.key(seed), 7)
    tower_images = scatter_about(arg_keys[0], (N_BLK * N_GRP * CAP, D), (D ** -0.5), 0.17675781, ((0, 512),))
    owners = draw_owners(jax.random.fold_in(arg_keys[6], 71), 0)
    counts = draw_counts(jax.random.fold_in(arg_keys[6], 71), 0)
    text = scatter_about(arg_keys[3], (TOTAL, D), (D ** -0.5), 0.17675781, ((0, 512),))
    logit_scale = jnp.clip(jax.random.uniform(arg_keys[4], (1,), jnp.float32, 8.0, 12.0), 8.0, 12.0)
    logit_bias = jnp.clip(jax.random.uniform(arg_keys[5], (1,), jnp.float32, -6.0, -3.0), -6.0, -3.0)
    return dict(tower_images=tower_images, owners=owners, counts=counts, text=text, logit_scale=logit_scale, logit_bias=logit_bias)


def unit_rows(values):
    wide = values.astype(jnp.float32)
    inverse = lax.rsqrt(lax.optimization_barrier(jnp.sum(wide * wide, axis=-1, keepdims=True)) + 1e-06)
    return (wide * inverse, inverse)

def unit_back(grad, unit, inverse):
    return (grad - unit * lax.optimization_barrier(jnp.sum(unit * grad, axis=-1, keepdims=True))) * inverse

def reference(tower_images, owners, counts, text, logit_scale, logit_bias):
    total = N_BLK * N_GRP * PAIRS_DEV
    slot = jnp.arange(N_BLK * N_GRP * CAP, dtype=jnp.int32)
    tower = slot // CAP
    live = slot % CAP < counts[tower]
    pair = tower // N_GRP * (N_GRP * PAIRS_DEV) + owners
    target = jnp.where(live, pair, total).astype(jnp.int32)
    images = jnp.zeros((total + 1, D), jnp.bfloat16).at[target].set(tower_images)[:total]
    image_unit, image_inv = unit_rows(images)
    text_unit, text_inv = unit_rows(text)
    image_low = lax.optimization_barrier(image_unit.astype(jnp.bfloat16)).astype(jnp.float32)
    text_low = lax.optimization_barrier(text_unit.astype(jnp.bfloat16)).astype(jnp.float32)
    scale = logit_scale[0]
    bias = logit_bias[0]
    block = math.gcd(total, 512)
    columns = jnp.arange(total, dtype=jnp.int32)

    def one_block(carry, index):
        start = (index * block).astype(jnp.int32)
        rows = lax.dynamic_slice_in_dim(image_low, start, block, 0)
        raw = jnp.dot(rows, text_low.T, precision=lax.Precision.HIGHEST)
        logits = scale * raw + bias
        row_ids = start + jnp.arange(block, dtype=jnp.int32)
        sign = jnp.where(row_ids[:, None] == columns[None, :], 1.0, -1.0).astype(jnp.float32)
        slope = -sign * jax.nn.sigmoid(-sign * logits)
        dscore = lax.optimization_barrier((scale * slope).astype(jnp.bfloat16)).astype(jnp.float32)
        image_part = jnp.dot(dscore, text_low, precision=lax.Precision.HIGHEST)
        carry = carry + jnp.dot(dscore.T, rows, precision=lax.Precision.HIGHEST)
        return (carry, image_part)
    text_unit_grad, parts = lax.scan(one_block, jnp.zeros((total, D), jnp.float32), jnp.arange(total // block, dtype=jnp.int32))
    image_unit_grad = parts.reshape(total, D)
    pair_grad = unit_back(image_unit_grad, image_unit, image_inv)
    picked = pair_grad[jnp.where(live, pair, 0).astype(jnp.int32)]
    image_grad = jnp.where(live[:, None], picked, jnp.zeros_like(picked))
    text_grad = unit_back(text_unit_grad, text_unit, text_inv)
    return (image_grad, text_grad)
```

```python
import jax
import jax.numpy as jnp
from jax import lax
from jax.experimental import pallas as pl
from jax.experimental.pallas import tpu as pltpu
from jax.sharding import PartitionSpec as P

MESH = pl.DeviceIdType.MESH
F32 = jnp.float32
BF16 = jnp.bfloat16
ORDER = (0, 1, -1, 2, -2, 3, -3, 4)
MESSAGES = 160


def pos(offset):
    return ORDER.index(4 if offset == -4 else offset)


def unit_rows(values):
    wide = values.astype(F32)
    inverse = lax.rsqrt(jnp.sum(wide * wide, axis=-1, keepdims=True) + 1e-06)
    return wide * inverse, inverse


def unit_back(grad, unit, inverse):
    return (grad - unit * jnp.sum(unit * grad, axis=-1, keepdims=True)) * inverse


def kernel(
    img_ref, own_ref, cnt_ref, text_ref, scale_ref, bias_ref,
    ig_ref, tg_ref,
    img, ids, id_own, id_sib, txt, dst, tu,
    gown, gsend, grecv, zs, zr_, ta, as_, ar_, axs, axr, tb, bxs, bxr, bys, byr,
    ssem, rsem,
):
    width = img_ref.shape[1]
    cap = img_ref.shape[0]
    pairs = text_ref.shape[0]
    blk = lax.axis_index("blk")
    grp = lax.axis_index("grp")
    x, y = blk % 4, (grp // 16) * 4 + blk // 4
    z, c = (grp // 2) % 8, grp % 2

    def device(x, y, z, c):
        return ((y % 4) * 4 + x, (y // 4) * 16 + z * 2 + c)

    zp, zm = device(x, y, (z + 1) % 8, c), device(x, y, (z + 7) % 8, c)
    yp, ym = device(x, (y + 1) % 8, z, c), device(x, (y + 7) % 8, z, c)
    core = device(x, y, z, 1 - c)
    xk = {k: device((x + k) % 4, y, z, c) for k in (1, 2, 3)}

    barrier = pltpu.get_barrier_semaphore()
    partners = [zp, zm, yp, ym, core, xk[1], xk[2], xk[3]]
    for p in partners:
        pl.semaphore_signal(barrier, inc=1, device_id=p, device_id_type=MESH)

    sent = []

    def send(src, dst_, where):
        i = len(sent)
        copy = pltpu.make_async_remote_copy(
            src_ref=src, dst_ref=dst_, send_sem=ssem.at[i], recv_sem=rsem.at[i],
            device_id=where, device_id_type=MESH,
        )
        copy.start()
        sent.append(copy)
        return copy

    def arrive(copies):
        for copy in copies:
            copy.wait_recv()

    live = lax.broadcasted_iota(jnp.int32, (cap, 1), 0) < cnt_ref[0]
    image_unit, image_inv = unit_rows(img_ref[...])
    img[0, 0] = jnp.where(live, image_unit, 0.0).astype(BF16)
    lane = lax.broadcasted_iota(jnp.int32, (8, 128), 1)
    slot = jnp.where(lane < cap, lane, lane - cap)
    id_own[...] = jnp.where(slot < cnt_ref[0], jnp.broadcast_to(own_ref[...], (8, 128)), -2)
    text_unit, text_inv = unit_rows(text_ref[...])
    tu[...] = jnp.zeros_like(tu)
    tu[0:pairs] = text_unit
    txt[0, 0, 0] = tu[0:16].astype(BF16)
    txt[1, 0, 0] = tu[16:32].astype(BF16)

    pl.semaphore_wait(barrier, len(partners))

    def z_hop(h):
        if h < 4:
            return [
                send(img.at[pos(1 - h), 0], img.at[pos(-h), 0], zp),
                send(img.at[pos(h - 1), 0], img.at[pos(h), 0], zm),
            ]
        return [
            send(img.at[pos(-3), 0, pl.ds(0, 32)], img.at[7, 0, pl.ds(0, 32)], zp),
            send(img.at[pos(3), 0, pl.ds(32, 32)], img.at[7, 0, pl.ds(32, 32)], zm),
        ]

    def id_hop(h):
        out = [send(ids.at[pos(1 - h)], ids.at[pos(-h)], zp)]
        if h < 4:
            out.append(send(ids.at[pos(h - 1)], ids.at[pos(h)], zm))
        return out

    def core_pass(first, n):
        return [send(img.at[pl.ds(first, n), 0], img.at[pl.ds(first, n), 1], core)]

    def a_across():
        return [send(txt.at[0, 0, 0], txt.at[0, 0, 4 - k], xk[k]) for k in (1, 2, 3)]

    def a_hop(h):
        if h < 4:
            return [
                send(txt.at[0, pos(1 - h)], txt.at[0, pos(-h)], yp),
                send(txt.at[0, pos(h - 1)], txt.at[0, pos(h)], ym),
            ]
        return [
            send(txt.at[0, pos(-3), pl.ds(0, 2)], txt.at[0, 7, pl.ds(0, 2)], yp),
            send(txt.at[0, pos(3), pl.ds(2, 2)], txt.at[0, 7, pl.ds(2, 2)], ym),
        ]

    def b_hop(h):
        out = [send(txt.at[1, pos(1 - h), 0], txt.at[1, pos(-h), 0], yp)]
        if h < 4:
            out.append(send(txt.at[1, pos(h - 1), 0], txt.at[1, pos(h), 0], ym))
        return out

    def b_across(first, n):
        return [
            send(txt.at[1, pl.ds(first, n), 0], txt.at[1, pl.ds(first, n), 4 - k], xk[k])
            for k in (1, 2, 3)
        ]

    scale = scale_ref[0]
    bias = bias_ref[0]

    def score(half, gt, gi):
        texts = txt[half, 2 * gt : 2 * gt + 2].reshape(128, width)
        images = img[2 * gi : 2 * gi + 2].reshape(4 * cap, width)
        raw = lax.dot_general(
            texts, images, (((1,), (1,)), ((), ())), preferred_element_type=F32
        )
        e = jnp.exp(-(scale * raw + bias))
        slope = 1.0 / (1.0 + e)
        if gt in (0, 3):
            at = 0 if gt == 0 else 64
            half_y = y // 4 if gt == 0 else 1 - y // 4
            owner = half_y * 16 + z * 2 + c
            row = lax.broadcasted_iota(jnp.int32, (128, 1), 0) - at
            named = (row >= 0) & (row < 16) & (row + 16 * half < pairs)
            row_id = jnp.where(named, owner * pairs + 16 * half + row, -1)
            column_id = jnp.concatenate([ids[2 * gi, 0:1], ids[2 * gi + 1, 0:1]], axis=1)
            slope = jnp.where(row_id == column_id, -e * slope, slope)
        dst[
            half * 512 + gt * 128 : half * 512 + gt * 128 + 128, gi * 256 : gi * 256 + 256
        ] = (scale * slope).astype(BF16)

    def scores(s):
        for gi in range(s + 1):
            for half in (0, 1):
                score(half, s, gi)
        for gt in range(s):
            for half in (0, 1):
                score(half, gt, s)

    zw = z_hop(1)
    idw = [send(id_own, id_sib, core)]
    aw = a_across()
    bw = b_hop(1)
    spans = ((0, 1), (1, 2), (3, 2), (5, 2), (7, 1))
    cw, bx = [core_pass(0, 1)], [b_across(0, 1)]
    arrive(idw)
    ids[0] = jnp.where(lane < cap, id_own[...], id_sib[...])
    idw = id_hop(1)
    arrive(aw)
    aw = a_hop(1)
    arrive(cw[0] + bx[0])
    for h in (1, 2, 3, 4):
        arrive(zw)
        if h < 4:
            zw = z_hop(h + 1)
        cw.append(core_pass(*spans[h]))
        arrive(bw)
        if h < 4:
            bw = b_hop(h + 1)
        bx.append(b_across(*spans[h]))
        arrive(idw)
        if h < 4:
            idw = id_hop(h + 1)
        arrive(aw)
        if h < 4:
            aw = a_hop(h + 1)
        if h > 1:
            arrive(cw[h - 1] + bx[h - 1])
            scores(h - 2)
    arrive(cw[4] + bx[4])
    scores(3)

    def image_part(gi):
        g = lax.dot_general(
            dst[:, gi * 256 : gi * 256 + 256], txt[...].reshape(1024, width),
            (((0,), (0,)), ((), ())), preferred_element_type=F32,
        ).reshape(2, 2, cap, width)
        gown[2 * gi : 2 * gi + 2] = g[:, 0]
        gsend[2 * gi : 2 * gi + 2] = g[:, 1].astype(BF16)
        return [send(gsend.at[pl.ds(2 * gi, 2)], grecv.at[pl.ds(2 * gi, 2)], core)]

    def text_part(half, gt):
        images = img[...].reshape(16 * cap, width)
        t = jnp.dot(
            dst[half * 512 + gt * 128 : half * 512 + gt * 128 + 128, :], images,
            preferred_element_type=F32,
        )
        if half == 0:
            ta[2 * gt : 2 * gt + 2] = t.reshape(2, 64, width)
            return []
        t = t.reshape(2, 4, 16, width)
        tb[2 * gt : 2 * gt + 2] = t[:, 0]
        bxs[2 * gt : 2 * gt + 2] = t[:, 1:].astype(BF16)
        two = pl.ds(2 * gt, 2)
        return [send(bxs.at[two, k - 1], bxr.at[two, k - 1], xk[k]) for k in (1, 2, 3)]

    def image_sum(p, j):
        rows = pl.ds(32 * j, 32)
        return gown[p, rows] + grecv[p, rows].astype(F32)

    def a_sum(p, j):
        return ta[p, pl.ds(32 * j, 32)]

    def hop_back(own, outs, ins, h, up, down):
        copies = []
        for side, sign, where in ((0, 1, up), (1, -1, down)):
            p = pos(sign * (5 - h))
            for j in (0, 1) if h > 1 else (side,):
                value = own(p, j)
                if h > 2 or (h == 2 and j == side):
                    value = value + ins[side, h - 2, j].astype(F32)
                outs[side, h - 1, j] = value.astype(BF16)
            if h > 1:
                copies.append(send(outs.at[side, h - 1], ins.at[side, h - 1], where))
            else:
                copies.append(send(outs.at[side, 0, side], ins.at[side, 0, side], where))
        return copies

    def b_sum(p):
        return tb[p] + bxr[p, 0].astype(F32) + bxr[p, 1].astype(F32) + bxr[p, 2].astype(F32)

    def b_back(h):
        copies = []
        for side, sign, where in ((0, 1, yp), (1, -1, ym)):
            if side == 1 and h == 1:
                continue
            value = b_sum(pos(sign * (5 - h)))
            if h > 1 + side:
                value = value + byr[side, h - 2].astype(F32)
            bys[side, h - 1] = value.astype(BF16)
            copies.append(send(bys.at[side, h - 1], byr.at[side, h - 1], where))
        return copies

    cores, across = {}, {}
    zw = aw = bw = []
    for h in (1, 2, 3, 4):
        g = 4 - h
        cores[g] = image_part(g)
        text_part(0, g)
        arrive(aw)
        aw = hop_back(a_sum, as_, ar_, h, yp, ym)
        across[g] = text_part(1, g)
        arrive(cores[g] + zw)
        zw = hop_back(image_sum, zs, zr_, h, zp, zm)
        arrive(across[g] + bw)
        bw = b_back(h)
    arrive(aw)
    own_a = [a_sum(0, j) + ar_[0, 3, j].astype(F32) + ar_[1, 3, j].astype(F32) for j in (0, 1)]
    for k in (1, 2, 3):
        axs[k - 1] = own_a[k // 2][16 * (k % 2) : 16 * (k % 2) + 16].astype(BF16)
    ax = [send(axs.at[k - 1], axr.at[k - 1], xk[k]) for k in (1, 2, 3)]
    arrive(zw)
    total = jnp.concatenate(
        [image_sum(0, j) + zr_[0, 3, j].astype(F32) + zr_[1, 3, j].astype(F32) for j in (0, 1)]
    )
    ig_ref[...] = jnp.where(live, unit_back(total, image_unit, image_inv), 0.0)
    arrive(bw)
    total_b = b_sum(0) + byr[0, 3].astype(F32) + byr[1, 3].astype(F32)
    arrive(ax)
    total_a = own_a[0][0:16]
    for k in range(3):
        total_a = total_a + axr[k].astype(F32)
    total = jnp.concatenate([total_a, total_b])[0:pairs]
    tg_ref[...] = unit_back(total, tu[0:pairs], text_inv)
    for copy in sent:
        copy.wait_send()


def shards(tower_images, owners, counts, text, logit_scale, logit_bias):
    cap, width = tower_images.shape
    pairs = text.shape[0]
    twice = jnp.concatenate([owners, owners]).reshape(1, 2 * cap)
    vmem = pl.BlockSpec(memory_space=pltpu.VMEM)
    smem = pl.BlockSpec(memory_space=pltpu.SMEM)
    V = pltpu.VMEM
    return pl.pallas_call(
        kernel,
        out_shape=(
            jax.ShapeDtypeStruct((cap, width), F32),
            jax.ShapeDtypeStruct((pairs, width), F32),
        ),
        in_specs=[vmem, vmem, smem, vmem, smem, smem],
        out_specs=(vmem, vmem),
        scratch_shapes=[
            V((8, 2, cap, width), BF16),
            V((8, 8, 128), jnp.int32),
            V((8, 128), jnp.int32),
            V((8, 128), jnp.int32),
            V((2, 8, 4, 16, width), BF16),
            V((1024, 1024), BF16),
            V((32, width), F32),
            V((8, cap, width), F32),
            V((8, cap, width), BF16),
            V((8, cap, width), BF16),
            V((2, 4, 2, 32, width), BF16),
            V((2, 4, 2, 32, width), BF16),
            V((8, 64, width), F32),
            V((2, 4, 2, 32, width), BF16),
            V((2, 4, 2, 32, width), BF16),
            V((3, 16, width), BF16),
            V((3, 16, width), BF16),
            V((8, 16, width), F32),
            V((8, 3, 16, width), BF16),
            V((8, 3, 16, width), BF16),
            V((2, 4, 16, width), BF16),
            V((2, 4, 16, width), BF16),
            pltpu.SemaphoreType.DMA((MESSAGES,)),
            pltpu.SemaphoreType.DMA((MESSAGES,)),
        ],
        compiler_params=pltpu.CompilerParams(
            collective_id=0, has_side_effects=True, vmem_limit_bytes=56 << 20
        ),
    )(tower_images, twice, counts, text, logit_scale, logit_bias)


def solution(mesh):
    split = P(("blk", "grp"))
    rows = P(("blk", "grp"), None)
    return jax.shard_map(
        shards, mesh=mesh, in_specs=(rows, split, split, rows, P(), P()), out_specs=(rows, rows),
        check_vma=False,
    )
```

```python
import jax
import jax.numpy as jnp
from jax import lax
from jax.experimental import pallas as pl
from jax.experimental.pallas import tpu as pltpu
from jax.sharding import PartitionSpec as P

MESH = pl.DeviceIdType.MESH
F32 = jnp.float32
BF16 = jnp.bfloat16
ORDER = (0, 1, -1, 2, -2, 3, -3, 4)
UNITS = 32
SEMAPHORES = 100


def pos(offset):
    return ORDER.index(4 if offset == -4 else offset)


def unit_rows(values):
    wide = values.astype(F32)
    inverse = lax.rsqrt(jnp.sum(wide * wide, axis=-1, keepdims=True) + 1e-06)
    return wide * inverse, inverse


def unit_back(grad, unit, inverse):
    return (grad - unit * jnp.sum(unit * grad, axis=-1, keepdims=True)) * inverse


def kernel(
    img_ref, own_ref, cnt_ref, text_ref, scale_ref, bias_ref,
    ig_ref, tg_ref,
    img, ids, id_own, id_sib, txt, dst, tu,
    gown, gsend, grecv, zs, zr_, ta, as_, ar_, axs, axr, tb, bxs, bxr, bys, byr,
    sems,
):
    width = img_ref.shape[1]
    cap = img_ref.shape[0]
    pairs = text_ref.shape[0]
    blk = lax.axis_index("blk")
    grp = lax.axis_index("grp")
    x, y = blk % 4, (grp // 16) * 4 + blk // 4
    z, c = (grp // 2) % 8, grp % 2

    def device(x, y, z, c):
        return ((y % 4) * 4 + x, (y // 4) * 16 + z * 2 + c)

    zp, zm = device(x, y, (z + 1) % 8, c), device(x, y, (z + 7) % 8, c)
    yp, ym = device(x, (y + 1) % 8, z, c), device(x, (y + 7) % 8, z, c)
    yp2, ym2 = device(x, (y + 2) % 8, z, c), device(x, (y + 6) % 8, z, c)
    core = device(x, y, z, 1 - c)
    xk = {k: device((x + k) % 4, y, z, c) for k in (1, 2, 3)}

    barrier = pltpu.get_barrier_semaphore()
    partners = [zp, zm, yp, ym, yp2, ym2, core, xk[1], xk[2], xk[3]]
    for p in partners:
        pl.semaphore_signal(barrier, inc=1, device_id=p, device_id_type=MESH)

    taken, outgoing = [0], []

    def group(kind=0):
        taken[0] += 1
        return [taken[0] - 1, 0, kind]

    def send(src, dst_, where, into, units):
        out = outgoing[-1] if outgoing else None
        if into[2]:
            out = id_sent
        elif out is None or out[1] + units > UNITS:
            out = group()
            outgoing.append(out)
        pltpu.make_async_remote_copy(
            src_ref=src, dst_ref=dst_, send_sem=sems.at[out[0]], recv_sem=sems.at[into[0]],
            device_id=where, device_id_type=MESH,
        ).start()
        out[1] += units
        into[1] += units

    def wait(done, arrived):
        whole = (ids if done[2] else ar_).at[pl.ds(0, done[1])]
        copy = pltpu.make_async_remote_copy(
            src_ref=whole, dst_ref=whole, send_sem=sems.at[done[0]], recv_sem=sems.at[done[0]],
            device_id=core, device_id_type=MESH,
        )
        copy.wait_recv() if arrived else copy.wait_send()

    def arrive(*groups):
        for g in groups:
            wait(g, True)

    id_sent = group(1)

    live = lax.broadcasted_iota(jnp.int32, (cap, 1), 0) < cnt_ref[0]
    image_unit, image_inv = unit_rows(img_ref[...])
    img[0, 0] = jnp.where(live, image_unit, 0.0).astype(BF16)
    lane = lax.broadcasted_iota(jnp.int32, (8, 128), 1)
    slot = jnp.where(lane < cap, lane, lane - cap)
    id_own[...] = jnp.where(slot < cnt_ref[0], jnp.broadcast_to(own_ref[...], (8, 128)), -2)
    text_unit, text_inv = unit_rows(text_ref[...])
    tu[...] = jnp.zeros_like(tu)
    tu[0:pairs] = text_unit
    txt[0, 0, 0] = tu[0:16].astype(BF16)
    txt[1, 0, 0] = tu[16:32].astype(BF16)

    pl.semaphore_wait(barrier, len(partners))

    def hops_of(side, q):
        return 4 if q // 2 == side else 3

    def z_hop(h, side, q, into):
        rows, sign = pl.ds(16 * q, 16), 1 - 2 * side
        send(
            img.at[pos(sign * (1 - h)), 0, rows], img.at[pos(-sign * h), 0, rows], (zp, zm)[side],
            into, 1,
        )

    def a_hop(h, side, q, into):
        sign = 1 - 2 * side
        src, to = txt.at[0, pos(sign * (1 - h)), q], txt.at[0, pos(-sign * h), q]
        send(src, to, (yp, ym)[side], into, 1)

    def id_hop(h):
        into = group(1)
        send(ids.at[pos(1 - h)], ids.at[pos(-h)], zp, into, 1)
        if h < 4:
            send(ids.at[pos(h - 1)], ids.at[pos(h)], zm, into, 1)
        return into

    def core_pass(first, n):
        into, span = group(), pl.ds(first, n)
        send(img.at[span, 0], img.at[span, 1], core, into, 4 * n)
        return into

    def b_copy(source, distance, into):
        where = {1: yp, -1: ym, 2: yp2, -2: ym2}[distance]
        send(txt.at[1, pos(source), 0], txt.at[1, pos(source - distance), 0], where, into, 1)

    def b_across(first, n):
        into, span = group(), pl.ds(first, n)
        for k in (1, 2, 3):
            send(txt.at[1, span, 0], txt.at[1, span, 4 - k], xk[k], into, n)
        return into

    scale = scale_ref[0]
    bias = bias_ref[0]

    def score(half, gt, gi):
        texts = txt[half, 2 * gt : 2 * gt + 2].reshape(128, width)
        images = img[2 * gi : 2 * gi + 2].reshape(4 * cap, width)
        raw = lax.dot_general(
            texts, images, (((1,), (1,)), ((), ())), preferred_element_type=F32
        )
        e = jnp.exp(-(scale * raw + bias))
        slope = 1.0 / (1.0 + e)
        if gt in (0, 3):
            at = 0 if gt == 0 else 64
            half_y = y // 4 if gt == 0 else 1 - y // 4
            owner = half_y * 16 + z * 2 + c
            row = lax.broadcasted_iota(jnp.int32, (128, 1), 0) - at
            named = (row >= 0) & (row < 16) & (row + 16 * half < pairs)
            row_id = jnp.where(named, owner * pairs + 16 * half + row, -1)
            column_id = jnp.concatenate([ids[2 * gi, 0:1], ids[2 * gi + 1, 0:1]], axis=1)
            slope = jnp.where(row_id == column_id, -e * slope, slope)
        dst[
            half * 512 + gt * 128 : half * 512 + gt * 128 + 128, gi * 256 : gi * 256 + 256
        ] = (scale * slope).astype(BF16)

    def scores(s):
        for gi in range(s + 1):
            for half in (0, 1):
                score(half, s, gi)
        for gt in range(s):
            for half in (0, 1):
                score(half, gt, s)

    both = (0, 1)
    chunks = range(4)
    order = (0, 3, 1, 2)
    ax = {}
    for k in (1, 2, 3):
        ax[4 - k] = group()
        send(txt.at[0, 0, 0], txt.at[0, 0, 4 - k], xk[k], ax[4 - k], 1)
    bw = group()
    for d in (1, -1, 2, -2):
        b_copy(0, d, bw)
    waits = {}

    def start(flow, h, q):
        hop = (z_hop, a_hop)[flow]
        for side in both:
            if h <= hops_of(side, q):
                key = (flow, h, q if h < 4 else min(q, 3 - q))
                if key not in waits:
                    waits[key] = group()
                hop(h, side, q, waits[key])

    for q in order:
        start(0, 1, q)
    start(1, 1, 0)
    idw = group(1)
    send(id_own, id_sib, core, idw, 1)
    bx = {0: b_across(0, 1)}
    cw = {0: core_pass(0, 1)}
    for q in (3, 1, 2):
        arrive(ax[q])
        start(1, 1, q)
    arrive(idw)
    ids[0] = jnp.where(lane < cap, id_own[...], id_sib[...])
    idw = id_hop(1)
    spans = ((0, 1), (1, 2), (3, 2), (5, 2), (7, 1))

    def forward(flow, h):
        if h < 4:
            for q in order:
                arrive(waits[flow, h, q])
                start(flow, h + 1, q)
        else:
            arrive(waits[flow, 4, 0], waits[flow, 4, 1])
        if flow == 0:
            cw[h] = core_pass(*spans[h])

    forward(0, 1)
    arrive(bw)
    bw = group()
    for source, d in ((-2, 1), (2, -1), (-2, 2)):
        b_copy(source, d, bw)
    bx[1] = b_across(1, 4)
    arrive(idw)
    idw = id_hop(2)
    forward(1, 1)
    forward(0, 2)
    arrive(bw)
    bx[2] = b_across(5, 3)
    arrive(idw)
    idw = id_hop(3)
    forward(1, 2)
    arrive(cw[0], cw[1], bx[0], bx[1])
    scores(0)
    forward(0, 3)
    arrive(idw)
    idw = id_hop(4)
    forward(1, 3)
    arrive(cw[2])
    scores(1)
    forward(0, 4)
    arrive(idw)
    arrive(cw[3], bx[2])
    scores(2)
    forward(1, 4)
    arrive(cw[4])
    scores(3)

    def image_part(gi):
        g = lax.dot_general(
            dst[:, gi * 256 : gi * 256 + 256], txt[...].reshape(1024, width),
            (((0,), (0,)), ((), ())), preferred_element_type=F32,
        ).reshape(2, 2, cap, width)
        gown[2 * gi : 2 * gi + 2] = g[:, 0]
        gsend[2 * gi : 2 * gi + 2] = g[:, 1].astype(BF16)
        into, two = group(), pl.ds(2 * gi, 2)
        send(gsend.at[two], grecv.at[two], core, into, 8)
        return into

    def text_part(half, gt):
        images = img[...].reshape(16 * cap, width)
        t = jnp.dot(
            dst[half * 512 + gt * 128 : half * 512 + gt * 128 + 128, :], images,
            preferred_element_type=F32,
        )
        if half == 0:
            ta[2 * gt : 2 * gt + 2] = t.reshape(2, 64, width)
            return None
        t = t.reshape(2, 4, 16, width)
        tb[2 * gt : 2 * gt + 2] = t[:, 0]
        bxs[2 * gt : 2 * gt + 2] = t[:, 1:].astype(BF16)
        into, two = group(), pl.ds(2 * gt, 2)
        for k in (1, 2, 3):
            send(bxs.at[two, k - 1], bxr.at[two, k - 1], xk[k], into, 2)
        return into

    def image_sum(p, q):
        rows = pl.ds(16 * q, 16)
        return gown[p, rows] + grecv[p, rows].astype(F32)

    def a_sum(p, q):
        return ta[p, pl.ds(16 * q, 16)]

    def at(side, h, q):
        return (side * 4 + h - 1) * 4 + q

    def hop_back(flow, h, q):
        own, outs, ins, ends = flows[flow]
        key = (flow, h, q if h > 1 else min(q, 3 - q))
        if h == 2 and q in (0, 1):
            arrive(waits[flow, 1, q])
        if h > 2:
            arrive(waits[flow, h - 1, q])
        if key not in waits:
            waits[key] = group()
        for side in both:
            if h > 4 - hops_of(side, q):
                value = own(pos((1 - 2 * side) * (5 - h)), q)
                if h - 1 > 4 - hops_of(side, q):
                    value = value + ins[at(side, h - 1, q)].astype(F32)
                spot = at(side, h, q)
                outs[spot] = value.astype(BF16)
                send(outs.at[spot], ins.at[spot], ends[side], waits[key], 1)

    def ring_total(flow, q):
        own, _, ins, _ = flows[flow]
        arrive(waits[flow, 4, q])
        return own(0, q) + ins[at(0, 4, q)].astype(F32) + ins[at(1, 4, q)].astype(F32)

    def b_sum(p):
        return tb[p] + bxr[p, 0].astype(F32) + bxr[p, 1].astype(F32) + bxr[p, 2].astype(F32)

    def b_back(slot, value, where, into):
        bys[slot] = value.astype(BF16)
        send(bys.at[slot], byr.at[slot], where, into, 1)

    def came(slot):
        return byr[slot].astype(F32)

    flows = ((image_sum, zs, zr_, (zp, zm)), (a_sum, as_, ar_, (yp, ym)))
    waits = {}
    cores, across = {}, {}
    for h in (1, 2, 3, 4):
        g = 4 - h
        cores[g] = image_part(g)
        text_part(0, g)
        across[g] = text_part(1, g)
        for q in order:
            hop_back(1, h, q)
        arrive(cores[g])
        for q in order:
            hop_back(0, h, q)
        if h == 2:
            arrive(across[3], across[2])
            far = group()
            b_back(0, b_sum(pos(-3)), ym, far)
            b_back(1, b_sum(pos(4)), ym2, far)
            b_back(2, b_sum(pos(3)), yp, far)
    axw = group()
    own_a = None
    for q in order:
        value = ring_total(1, q)
        if q == 0:
            own_a = value
        else:
            axs[q - 1] = value.astype(BF16)
            send(axs.at[q - 1], axr.at[q - 1], xk[q], axw, 1)
    arrive(across[1], across[0], far)
    near = group()
    b_back(3, b_sum(pos(-2)) + came(0) + came(1), ym2, near)
    b_back(4, b_sum(pos(2)) + came(2), yp2, near)
    b_back(5, b_sum(pos(-1)), ym, near)
    b_back(6, b_sum(pos(1)), yp, near)
    total = jnp.concatenate([ring_total(0, q) for q in chunks])
    ig_ref[...] = jnp.where(live, unit_back(total, image_unit, image_inv), 0.0)
    arrive(axw)
    total_a = own_a
    for k in range(3):
        total_a = total_a + axr[k].astype(F32)
    arrive(near)
    total_b = b_sum(0) + came(3) + came(4) + came(5) + came(6)
    total = jnp.concatenate([total_a, total_b])[0:pairs]
    tg_ref[...] = unit_back(total, tu[0:pairs], text_inv)
    for g in outgoing + [id_sent]:
        wait(g, False)


def shards(tower_images, owners, counts, text, logit_scale, logit_bias):
    cap, width = tower_images.shape
    pairs = text.shape[0]
    twice = jnp.concatenate([owners, owners]).reshape(1, 2 * cap)
    vmem = pl.BlockSpec(memory_space=pltpu.VMEM)
    smem = pl.BlockSpec(memory_space=pltpu.SMEM)
    V = pltpu.VMEM
    return pl.pallas_call(
        kernel,
        out_shape=(
            jax.ShapeDtypeStruct((cap, width), F32),
            jax.ShapeDtypeStruct((pairs, width), F32),
        ),
        in_specs=[vmem, vmem, smem, vmem, smem, smem],
        out_specs=(vmem, vmem),
        scratch_shapes=[
            V((8, 2, cap, width), BF16),
            V((8, 8, 128), jnp.int32),
            V((8, 128), jnp.int32),
            V((8, 128), jnp.int32),
            V((2, 8, 4, 16, width), BF16),
            V((1024, 1024), BF16),
            V((32, width), F32),
            V((8, cap, width), F32),
            V((8, cap, width), BF16),
            V((8, cap, width), BF16),
            V((32, 16, width), BF16),
            V((32, 16, width), BF16),
            V((8, 64, width), F32),
            V((32, 16, width), BF16),
            V((32, 16, width), BF16),
            V((3, 16, width), BF16),
            V((3, 16, width), BF16),
            V((8, 16, width), F32),
            V((8, 3, 16, width), BF16),
            V((8, 3, 16, width), BF16),
            V((7, 16, width), BF16),
            V((7, 16, width), BF16),
            pltpu.SemaphoreType.DMA((SEMAPHORES,)),
        ],
        compiler_params=pltpu.CompilerParams(
            collective_id=0, has_side_effects=True, vmem_limit_bytes=56 << 20
        ),
    )(tower_images, twice, counts, text, logit_scale, logit_bias)


def solution(mesh):
    split = P(("blk", "grp"))
    rows = P(("blk", "grp"), None)
    return jax.shard_map(
        shards, mesh=mesh, in_specs=(rows, split, split, rows, P(), P()), out_specs=(rows, rows),
        check_vma=False,
    )
```

```python
import jax
import jax.numpy as jnp
from jax import lax
from jax.experimental import pallas as pl
from jax.experimental.pallas import tpu as pltpu
from jax.sharding import PartitionSpec as P

MESH = pl.DeviceIdType.MESH
F32 = jnp.float32
BF16 = jnp.bfloat16
ORDER = (0, 1, -1, 2, -2, 3, -3, 4)
UNITS = 32
PACKED = 896
BASE = (16, 0)
SEMAPHORES = 108


def pos(offset):
    return ORDER.index(4 if offset == -4 else offset)


def unit_rows(values):
    wide = values.astype(F32)
    inverse = lax.rsqrt(jnp.sum(wide * wide, axis=-1, keepdims=True) + 1e-06)
    return wide * inverse, inverse


def unit_back(grad, unit, inverse):
    return (grad - unit * jnp.sum(unit * grad, axis=-1, keepdims=True)) * inverse


def pack(rows):
    low = lax.broadcasted_iota(jnp.int32, (8, 128), 0) < 4
    spare = []
    for tile in (7, 8):
        lanes = slice(128 * tile, 128 * tile + 128)
        up, down = rows[0:8, lanes], rows[8:16, lanes]
        spare += [pltpu.roll(up, 4, 0), up, pltpu.roll(down, 4, 0)]
    spare.append(jnp.zeros((8, 128), F32))
    second = [
        jnp.where(low, rows[8:16, 128 * m : 128 * m + 128], spare[m]) for m in range(7)
    ]
    return jnp.concatenate([rows[0:8, 0:PACKED], jnp.concatenate(second, axis=1)], axis=0)


def unpack(rows):
    low = lax.broadcasted_iota(jnp.int32, (8, 128), 0) < 4
    zero = jnp.zeros((8, 128), F32)
    part = [rows[8:16, 128 * m : 128 * m + 128] for m in range(7)]
    up, down = [rows[0:8]], [jnp.where(low, p, zero) for p in part]
    for m in (0, 3):
        up.append(jnp.where(low, pltpu.roll(part[m], 4, 0), part[m + 1]))
        down.append(jnp.where(low, pltpu.roll(part[m + 2], 4, 0), zero))
    return jnp.concatenate([jnp.concatenate(up, axis=1), jnp.concatenate(down, axis=1)], axis=0)


def kernel(
    img_ref, own_ref, cnt_ref, text_ref, scale_ref, bias_ref,
    ig_ref, tg_ref,
    img, ids, id_own, id_sib, txt, pk, dst, tu,
    gown, gsend, grecv, zs, zr_, ta, as_, ar_, axs, axr, tb, bxs, bxr, bys, byr,
    sems,
):
    width = img_ref.shape[1]
    cap = img_ref.shape[0]
    pairs = text_ref.shape[0]
    blk = lax.axis_index("blk")
    grp = lax.axis_index("grp")
    x, y = blk % 4, (grp // 16) * 4 + blk // 4
    z, c = (grp // 2) % 8, grp % 2

    def device(x, y, z, c):
        return ((y % 4) * 4 + x, (y // 4) * 16 + z * 2 + c)

    zp, zm = device(x, y, (z + 1) % 8, c), device(x, y, (z + 7) % 8, c)
    yp, ym = device(x, (y + 1) % 8, z, c), device(x, (y + 7) % 8, z, c)
    yp2, ym2 = device(x, (y + 2) % 8, z, c), device(x, (y + 6) % 8, z, c)
    core = device(x, y, z, 1 - c)
    xk = {k: device((x + k) % 4, y, z, c) for k in (1, 2, 3)}

    barrier = pltpu.get_barrier_semaphore()
    partners = [zp, zm, yp, ym, yp2, ym2, core, xk[1], xk[2], xk[3]]
    for p in partners:
        pl.semaphore_signal(barrier, inc=1, device_id=p, device_id_type=MESH)

    taken, outgoing = [0], []
    full = {0: zr_, 1: ids, 2: pk}

    def group(kind=0):
        taken[0] += 1
        return [taken[0] - 1, 0, kind]

    def send(src, dst_, where, into, units):
        same = [g for g in outgoing if g[2] == into[2]]
        if same and same[-1][1] + units <= UNITS:
            out = same[-1]
        else:
            out = group(into[2])
            outgoing.append(out)
        pltpu.make_async_remote_copy(
            src_ref=src, dst_ref=dst_, send_sem=sems.at[out[0]], recv_sem=sems.at[into[0]],
            device_id=where, device_id_type=MESH,
        ).start()
        out[1] += units
        into[1] += units

    def wait(done, arrived):
        whole = full[done[2]].at[pl.ds(0, int(done[1]))]
        copy = pltpu.make_async_remote_copy(
            src_ref=whole, dst_ref=whole, send_sem=sems.at[done[0]], recv_sem=sems.at[done[0]],
            device_id=core, device_id_type=MESH,
        )
        copy.wait_recv() if arrived else copy.wait_send()

    def arrive(*groups):
        for g in groups:
            wait(g, True)

    live = lax.broadcasted_iota(jnp.int32, (cap, 1), 0) < cnt_ref[0]
    image_unit, image_inv = unit_rows(img_ref[...])
    img[0, 0] = jnp.where(live, image_unit, 0.0).astype(BF16)
    lane = lax.broadcasted_iota(jnp.int32, (8, 128), 1)
    slot = jnp.where(lane < cap, lane, lane - cap)
    id_own[...] = jnp.zeros_like(id_own)
    id_own[:, 0:cap] = jnp.broadcast_to(own_ref[...], (8, cap))
    twice = jnp.where(lane < cap, id_own[...], pltpu.roll(id_own[...], cap, 1))
    id_own[...] = jnp.where(slot < cnt_ref[0], twice, -2)
    text_unit, text_inv = unit_rows(text_ref[...])
    tu[...] = jnp.zeros_like(tu)
    tu[0:pairs] = text_unit
    txt[1, 0, 0] = tu[0:16].astype(BF16)
    pk[0] = pack(tu[16:32]).astype(BF16)

    pl.semaphore_wait(barrier, len(partners))

    both = (0, 1)
    cut = 128 * ((width // 128 + 1) // 2)
    left, right = pl.ds(0, cut), pl.ds(cut, width - cut)

    def hops_of(side, q):
        return 4 if q // 2 == side else 3

    def z_hop(h, side, q, into):
        rows, sign = pl.ds(16 * q, 16), 1 - 2 * side
        send(
            img.at[pos(sign * (1 - h)), 0, rows], img.at[pos(-sign * h), 0, rows], (zp, zm)[side],
            into, 1,
        )

    def a_hop(h, side, q, into):
        sign = 1 - 2 * side
        src, to = pk.at[4 * pos(sign * (1 - h)) + q], pk.at[4 * pos(-sign * h) + q]
        send(src, to, (yp, ym)[side], into, 1)

    def id_hop(h):
        into = group(1)
        send(ids.at[pos(1 - h)], ids.at[pos(-h)], zp, into, 1)
        if h < 4:
            send(ids.at[pos(h - 1)], ids.at[pos(h)], zm, into, 1)
        return into

    def core_pass(first, n):
        into, span = group(), pl.ds(first, n)
        send(img.at[span, 0], img.at[span, 1], core, into, 4 * n)
        return into

    def b_hop(h):
        into = group()
        if h < 4:
            send(txt.at[1, pos(1 - h), 0], txt.at[1, pos(-h), 0], yp, into, 1)
            send(txt.at[1, pos(h - 1), 0], txt.at[1, pos(h), 0], ym, into, 1)
        else:
            for source, where, lanes in ((-3, yp, left), (3, ym, right)):
                send(txt.at[1, pos(source), 0, :, lanes], txt.at[1, 7, 0, :, lanes], where, into, 0.5)
        return into

    def b_across(first, n, far):
        into, span = group(), pl.ds(first, n)
        for k in (1, 3) + ((2,) if far else ()):
            send(txt.at[1, span, 0], txt.at[1, span, 4 - k], xk[k], into, n)
        return into

    def b_onward(first, n):
        into, span = group(), pl.ds(first, n)
        for source, k, lanes in ((3, 1, left), (1, 3, right)):
            send(
                txt.at[1, span, source, :, lanes], txt.at[1, span, 2, :, lanes], xk[k], into, n / 2
            )
        return into

    scale = scale_ref[0]
    bias = bias_ref[0]

    def score(half, gt, gi):
        texts = txt[half, 2 * gt : 2 * gt + 2].reshape(128, width)
        images = img[2 * gi : 2 * gi + 2].reshape(4 * cap, width)
        raw = lax.dot_general(
            texts, images, (((1,), (1,)), ((), ())), preferred_element_type=F32
        )
        e = jnp.exp(-(scale * raw + bias))
        slope = 1.0 / (1.0 + e)
        if gt in (0, 3):
            at = 0 if gt == 0 else 64
            half_y = y // 4 if gt == 0 else 1 - y // 4
            owner = half_y * 16 + z * 2 + c
            row = lax.broadcasted_iota(jnp.int32, (128, 1), 0) - at
            named = (row >= 0) & (row < 16) & (row + BASE[half] < pairs)
            row_id = jnp.where(named, owner * pairs + BASE[half] + row, -1)
            column_id = jnp.concatenate([ids[2 * gi, 0:1], ids[2 * gi + 1, 0:1]], axis=1)
            slope = jnp.where(row_id == column_id, -e * slope, slope)
        dst[
            half * 512 + gt * 128 : half * 512 + gt * 128 + 128, gi * 256 : gi * 256 + 256
        ] = (scale * slope).astype(BF16)

    def scores(tiles):
        for half, gt, gi in tiles:
            score(half, gt, gi)

    def known(s):
        return [(half, s, gi) for gi in range(s + 1) for half in both] + [
            (half, gt, s) for gt in range(s) for half in both
        ]

    chunks = range(4)
    order = (0, 3, 1, 2)
    ax = {}
    for k in (1, 2, 3):
        ax[4 - k] = group(2)
        send(pk.at[0], pk.at[4 - k], xk[k], ax[4 - k], 1)
    bw = b_hop(1)
    waits = {}

    def start(flow, h, q):
        hop = (z_hop, a_hop)[flow]
        for side in both:
            if h <= hops_of(side, q):
                key = (flow, h, q if h < 4 else min(q, 3 - q))
                if key not in waits:
                    waits[key] = group(2 * flow)
                hop(h, side, q, waits[key])

    for q in order:
        start(0, 1, q)
    start(1, 1, 0)
    idw = group(1)
    send(id_own, id_sib, core, idw, 1)
    bx = {0: b_across(0, 1, False)}
    by = {}
    cw = {0: core_pass(0, 1)}
    for q in (3, 1, 2):
        arrive(ax[q])
        start(1, 1, q)
    arrive(idw)
    ids[0] = jnp.where(lane < cap, id_own[...], id_sib[...])
    idw = id_hop(1)
    spans = ((0, 1), (1, 2), (3, 2), (5, 2), (7, 1))

    def spread(p):
        for k in chunks:
            txt[0, p, k] = unpack(pk[4 * p + k].astype(F32)).astype(BF16)

    def onward(h):
        arrive(bx[h])
        by[h] = b_onward(*spans[h])

    def forward(flow, h):
        if h < 4:
            for q in order:
                arrive(waits[flow, h, q])
                start(flow, h + 1, q)
        else:
            arrive(waits[flow, 4, 0], waits[flow, 4, 1])
        if flow == 0:
            cw[h] = core_pass(*spans[h])
        else:
            for p in (pos(h), pos(-h)) if h < 4 else (7,):
                spread(p)

    def b_forward(h):
        arrive(bw_[0])
        if h < 4:
            bw_[0] = b_hop(h + 1)
        bx[h] = b_across(*spans[h], h > 2)

    bw_ = [bw]
    b_forward(1)
    onward(0)
    spread(0)
    forward(0, 1)
    arrive(idw)
    idw = id_hop(2)
    forward(1, 1)
    onward(1)
    b_forward(2)
    forward(0, 2)
    arrive(idw)
    idw = id_hop(3)
    forward(1, 2)
    onward(2)
    b_forward(3)
    arrive(cw[0], cw[1], by[0], by[1])
    scores(known(0))
    forward(0, 3)
    arrive(idw)
    idw = id_hop(4)
    forward(1, 3)
    b_forward(4)
    arrive(cw[2], by[2])
    scores(known(1))
    forward(0, 4)
    arrive(idw)
    arrive(cw[3], bx[3])
    scores(known(2))
    arrive(cw[4], bx[4])
    last = known(3)
    scores([t for t in last if t[:2] != (0, 3)])
    forward(1, 4)
    scores([t for t in last if t[:2] == (0, 3)])

    def image_part(gi):
        g = lax.dot_general(
            dst[:, gi * 256 : gi * 256 + 256], txt[...].reshape(1024, width),
            (((0,), (0,)), ((), ())), preferred_element_type=F32,
        ).reshape(2, 2, cap, width)
        gown[2 * gi : 2 * gi + 2] = g[:, 0]
        gsend[2 * gi : 2 * gi + 2] = g[:, 1].astype(BF16)
        into, two = group(), pl.ds(2 * gi, 2)
        send(gsend.at[two], grecv.at[two], core, into, 8)
        return into

    def text_part(half, gt):
        images = img[...].reshape(16 * cap, width)
        t = jnp.dot(
            dst[half * 512 + gt * 128 : half * 512 + gt * 128 + 128, :], images,
            preferred_element_type=F32,
        )
        if half == 0:
            for m in range(8):
                ta[8 * gt + m] = pack(t[16 * m : 16 * m + 16])
            return None
        t = t.reshape(2, 4, 16, width)
        tb[2 * gt : 2 * gt + 2] = t[:, 0]
        bxs[2 * gt : 2 * gt + 2] = t[:, 1:].astype(BF16)
        into, two = group(), pl.ds(2 * gt, 2)
        for k in (1, 2, 3):
            send(bxs.at[two, k - 1], bxr.at[two, k - 1], xk[k], into, 2)
        return into

    def image_sum(p, q):
        rows = pl.ds(16 * q, 16)
        return gown[p, rows] + grecv[p, rows].astype(F32)

    def a_sum(p, q):
        return ta[4 * p + q]

    def at(side, h, q):
        return (side * 4 + h - 1) * 4 + q

    def hop_back(flow, h, side, q):
        own, outs, ins, ends = flows[flow]
        first = 5 - hops_of(side, q)
        if h < first:
            return
        key = (flow, h, q if h > 1 else min(q, 3 - q))
        if key not in waits:
            waits[key] = group(2 * flow)
        value = own(pos((1 - 2 * side) * (5 - h)), q)
        if h > first:
            value = value + ins[at(side, h - 1, q)].astype(F32)
        spot = at(side, h, q)
        outs[spot] = value.astype(BF16)
        send(outs.at[spot], ins.at[spot], ends[side], waits[key], 1)

    def begin(flow, h):
        for q in order:
            for side in both:
                if 5 - hops_of(side, q) == h:
                    hop_back(flow, h, side, q)

    def carry(flow, h):
        for q in order:
            if h == 2:
                if q in (0, 1):
                    arrive(waits[flow, 1, q])
                hop_back(flow, 2, q // 2, q)
            else:
                arrive(waits[flow, h - 1, q])
                for side in both:
                    hop_back(flow, h, side, q)

    def ring_total(flow, q):
        own, _, ins, _ = flows[flow]
        arrive(waits[flow, 4, q])
        return own(0, q) + ins[at(0, 4, q)].astype(F32) + ins[at(1, 4, q)].astype(F32)

    def b_sum(p):
        return tb[p] + bxr[p, 0].astype(F32) + bxr[p, 1].astype(F32) + bxr[p, 2].astype(F32)

    def b_back(slot, value, where, into):
        bys[slot] = value.astype(BF16)
        send(bys.at[slot], byr.at[slot], where, into, 1)

    def b_far():
        far = group()
        b_back(0, b_sum(pos(-3)), ym, far)
        b_back(2, b_sum(pos(3)), yp, far)
        bys[1] = b_sum(pos(4)).astype(BF16)
        for where, lanes in ((ym2, left), (yp2, right)):
            send(bys.at[1, :, lanes], byr.at[1, :, lanes], where, far, 0.5)
        return far

    def came(slot):
        return byr[slot].astype(F32)

    leftish = lax.broadcasted_iota(jnp.int32, (16, width), 1) < cut
    flows = ((image_sum, zs, zr_, (zp, zm)), (a_sum, as_, ar_, (yp, ym)))
    waits = {}
    cores, across = {}, {}
    text_part(0, 3)
    begin(1, 1)
    cores[3] = image_part(3)
    across[3] = text_part(1, 3)
    text_part(0, 2)
    begin(1, 2)
    cores[2] = image_part(2)
    arrive(cores[3])
    begin(0, 1)
    across[2] = text_part(1, 2)
    arrive(cores[2])
    begin(0, 2)
    carry(1, 2)
    text_part(0, 1)
    across[1] = text_part(1, 1)
    cores[1] = image_part(1)
    carry(0, 2)
    text_part(0, 0)
    across[0] = text_part(1, 0)
    carry(1, 3)
    arrive(cores[1])
    cores[0] = image_part(0)
    carry(0, 3)
    arrive(across[3], across[2])
    far = b_far()
    carry(1, 4)
    arrive(cores[0])
    carry(0, 4)
    arrive(across[1], across[0], far)
    near = group()
    wide = came(1)
    zeros = jnp.zeros((16, width), F32)
    b_back(3, b_sum(pos(-2)) + came(0) + jnp.where(leftish, wide, zeros), ym2, near)
    b_back(4, b_sum(pos(2)) + came(2) + jnp.where(leftish, zeros, wide), yp2, near)
    b_back(5, b_sum(pos(-1)), ym, near)
    b_back(6, b_sum(pos(1)), yp, near)
    axw = group(2)
    own_a = None
    for q in order:
        value = ring_total(1, q)
        if q == 0:
            own_a = value
        else:
            axs[q - 1] = value.astype(BF16)
            send(axs.at[q - 1], axr.at[q - 1], xk[q], axw, 1)
    total = jnp.concatenate([ring_total(0, q) for q in chunks])
    ig_ref[...] = jnp.where(live, unit_back(total, image_unit, image_inv), 0.0)
    arrive(axw)
    total_a = own_a
    for k in range(3):
        total_a = total_a + axr[k].astype(F32)
    arrive(near)
    total_b = b_sum(0) + came(3) + came(4) + came(5) + came(6)
    total = jnp.concatenate([total_b, unpack(total_a)])[0:pairs]
    tg_ref[...] = unit_back(total, tu[0:pairs], text_inv)
    for g in outgoing:
        wait(g, False)


def hand_out(a_ref, b_ref, c_ref, d_ref):
    c_ref[...] = a_ref[...]
    d_ref[...] = b_ref[...]


def shards(tower_images, owners, counts, text, logit_scale, logit_bias):
    cap, width = tower_images.shape
    pairs = text.shape[0]
    vmem = pl.BlockSpec(memory_space=pltpu.VMEM)
    smem = pl.BlockSpec(memory_space=pltpu.SMEM)
    V = pltpu.VMEM
    grads = pl.pallas_call(
        kernel,
        out_shape=(
            jax.ShapeDtypeStruct((cap, width), F32),
            jax.ShapeDtypeStruct((pairs, width), F32),
        ),
        in_specs=[vmem, vmem, smem, vmem, smem, smem],
        out_specs=(vmem, vmem),
        scratch_shapes=[
            V((8, 2, cap, width), BF16),
            V((8, 8, 128), jnp.int32),
            V((8, 128), jnp.int32),
            V((8, 128), jnp.int32),
            V((2, 8, 4, 16, width), BF16),
            V((32, 16, PACKED), BF16),
            V((1024, 1024), BF16),
            V((32, width), F32),
            V((8, cap, width), F32),
            V((8, cap, width), BF16),
            V((8, cap, width), BF16),
            V((32, 16, width), BF16),
            V((32, 16, width), BF16),
            V((32, 16, PACKED), F32),
            V((32, 16, PACKED), BF16),
            V((32, 16, PACKED), BF16),
            V((3, 16, PACKED), BF16),
            V((3, 16, PACKED), BF16),
            V((8, 16, width), F32),
            V((8, 3, 16, width), BF16),
            V((8, 3, 16, width), BF16),
            V((7, 16, width), BF16),
            V((7, 16, width), BF16),
            pltpu.SemaphoreType.DMA((SEMAPHORES,)),
        ],
        compiler_params=pltpu.CompilerParams(
            collective_id=0, has_side_effects=True, vmem_limit_bytes=56 << 20
        ),
    )(tower_images, owners.reshape(1, cap), counts, text, logit_scale, logit_bias)
    return pl.pallas_call(
        hand_out,
        out_shape=tuple(jax.ShapeDtypeStruct(g.shape, g.dtype) for g in grads),
        in_specs=[vmem, vmem],
        out_specs=(vmem, vmem),
    )(*grads)


def solution(mesh):
    split = P(("blk", "grp"))
    rows = P(("blk", "grp"), None)
    return jax.shard_map(
        shards, mesh=mesh, in_specs=(rows, split, split, rows, P(), P()), out_specs=(rows, rows),
        check_vma=False,
    )
```

```python
import jax
import jax.numpy as jnp
from jax import lax
from jax.experimental import pallas as pl
from jax.experimental.pallas import tpu as pltpu
from jax.sharding import PartitionSpec as P

MESH = pl.DeviceIdType.MESH
F32 = jnp.float32
BF16 = jnp.bfloat16
ORDER = (0, 1, -1, 2, -2, 3, -3, 4)
UNITS = 32
PACKED = 896
BASE = (16, 0)
SEMAPHORES = 112


def pos(offset):
    return ORDER.index(4 if offset == -4 else offset)


def unit_rows(values):
    wide = values.astype(F32)
    inverse = lax.rsqrt(jnp.sum(wide * wide, axis=-1, keepdims=True) + 1e-06)
    return wide * inverse, inverse


def unit_back(grad, unit, inverse):
    return (grad - unit * jnp.sum(unit * grad, axis=-1, keepdims=True)) * inverse


def pack(rows):
    low = lax.broadcasted_iota(jnp.int32, (8, 128), 0) < 4
    spare = []
    for tile in (7, 8):
        lanes = slice(128 * tile, 128 * tile + 128)
        up, down = rows[0:8, lanes], rows[8:16, lanes]
        spare += [pltpu.roll(up, 4, 0), up, pltpu.roll(down, 4, 0)]
    spare.append(jnp.zeros((8, 128), F32))
    second = [
        jnp.where(low, rows[8:16, 128 * m : 128 * m + 128], spare[m]) for m in range(7)
    ]
    return jnp.concatenate([rows[0:8, 0:PACKED], jnp.concatenate(second, axis=1)], axis=0)


def unpack(rows):
    low = lax.broadcasted_iota(jnp.int32, (8, 128), 0) < 4
    zero = jnp.zeros((8, 128), F32)
    part = [rows[8:16, 128 * m : 128 * m + 128] for m in range(7)]
    up, down = [rows[0:8]], [jnp.where(low, p, zero) for p in part]
    for m in (0, 3):
        up.append(jnp.where(low, pltpu.roll(part[m], 4, 0), part[m + 1]))
        down.append(jnp.where(low, pltpu.roll(part[m + 2], 4, 0), zero))
    return jnp.concatenate([jnp.concatenate(up, axis=1), jnp.concatenate(down, axis=1)], axis=0)


def kernel(
    img_ref, own_ref, cnt_ref, text_ref, scale_ref, bias_ref,
    ig_ref, tg_ref,
    img, ids, id_own, id_sib, txt, pk, dst, tu,
    gown, gsend, grecv, zs, zr_, ta, as_, ar_, axs, axr, tb, bxs, bxr, bys, byr,
    sems,
):
    width = img_ref.shape[1]
    cap = img_ref.shape[0]
    pairs = text_ref.shape[0]
    blk = lax.axis_index("blk")
    grp = lax.axis_index("grp")
    x, y = blk % 4, (grp // 16) * 4 + blk // 4
    z, c = (grp // 2) % 8, grp % 2

    def device(x, y, z, c):
        return ((y % 4) * 4 + x, (y // 4) * 16 + z * 2 + c)

    zp, zm = device(x, y, (z + 1) % 8, c), device(x, y, (z + 7) % 8, c)
    yp, ym = device(x, (y + 1) % 8, z, c), device(x, (y + 7) % 8, z, c)
    yp2, ym2 = device(x, (y + 2) % 8, z, c), device(x, (y + 6) % 8, z, c)
    core = device(x, y, z, 1 - c)
    xk = {k: device((x + k) % 4, y, z, c) for k in (1, 2, 3)}

    barrier = pltpu.get_barrier_semaphore()
    partners = [zp, zm, yp, ym, yp2, ym2, core, xk[1], xk[2], xk[3]]
    for p in partners:
        pl.semaphore_signal(barrier, inc=1, device_id=p, device_id_type=MESH)

    taken, outgoing = [0], []
    full = {0: zr_, 1: ids, 2: pk}

    def group(kind=0):
        taken[0] += 1
        return [taken[0] - 1, 0, kind]

    def send(src, dst_, where, into, units):
        same = [g for g in outgoing if g[2] == into[2]]
        if same and same[-1][1] + units <= UNITS:
            out = same[-1]
        else:
            out = group(into[2])
            outgoing.append(out)
        pltpu.make_async_remote_copy(
            src_ref=src, dst_ref=dst_, send_sem=sems.at[out[0]], recv_sem=sems.at[into[0]],
            device_id=where, device_id_type=MESH,
        ).start()
        out[1] += units
        into[1] += units

    def wait(done, arrived):
        whole = full[done[2]].at[pl.ds(0, int(done[1]))]
        copy = pltpu.make_async_remote_copy(
            src_ref=whole, dst_ref=whole, send_sem=sems.at[done[0]], recv_sem=sems.at[done[0]],
            device_id=core, device_id_type=MESH,
        )
        copy.wait_recv() if arrived else copy.wait_send()

    def arrive(*groups):
        for g in groups:
            wait(g, True)

    live = lax.broadcasted_iota(jnp.int32, (cap, 1), 0) < cnt_ref[...]
    image_unit, image_inv = unit_rows(img_ref[...])
    img[0, 0] = jnp.where(live, image_unit, 0.0).astype(BF16)
    lane = lax.broadcasted_iota(jnp.int32, (8, 128), 1)
    slot = jnp.where(lane < cap, lane, lane - cap)
    id_own[...] = jnp.zeros_like(id_own)
    id_own[:, 0:cap] = jnp.broadcast_to(own_ref[...], (8, cap))
    twice = jnp.where(lane < cap, id_own[...], pltpu.roll(id_own[...], cap, 1))
    id_own[...] = jnp.where(slot < cnt_ref[...], twice, -2)
    text_unit, text_inv = unit_rows(text_ref[...])
    tu[...] = jnp.zeros_like(tu)
    tu[0:pairs] = text_unit
    txt[1, 0, 0] = tu[0:16].astype(BF16)
    pk[0] = pack(tu[16:32]).astype(BF16)

    pl.semaphore_wait(barrier, len(partners))

    both = (0, 1)
    cut = 128 * ((width // 128 + 1) // 2)
    left, right = pl.ds(0, cut), pl.ds(cut, width - cut)

    def hops_of(side, q):
        return 4 if q // 2 == side else 3

    def z_hop(h, side, q, into):
        rows, sign = pl.ds(16 * q, 16), 1 - 2 * side
        send(
            img.at[pos(sign * (1 - h)), 0, rows], img.at[pos(-sign * h), 0, rows], (zp, zm)[side],
            into, 1,
        )

    def a_hop(h, side, q, into):
        sign = 1 - 2 * side
        src, to = pk.at[4 * pos(sign * (1 - h)) + q], pk.at[4 * pos(-sign * h) + q]
        send(src, to, (yp, ym)[side], into, 1)

    def id_hop(h):
        into = group(1)
        send(ids.at[pos(1 - h)], ids.at[pos(-h)], zp, into, 1)
        if h < 4:
            send(ids.at[pos(h - 1)], ids.at[pos(h)], zm, into, 1)
        return into

    def core_pass(first, n):
        into, span = group(), pl.ds(first, n)
        send(img.at[span, 0], img.at[span, 1], core, into, 4 * n)
        return into

    def b_hop(h):
        into = group()
        send(txt.at[1, pos(1 - h), 0], txt.at[1, pos(-h), 0], yp, into, 1)
        send(txt.at[1, pos(h - 1), 0], txt.at[1, pos(h), 0], ym, into, 1)
        if h == 3:
            for source, where, lanes in ((-2, yp2, left), (2, ym2, right)):
                src, to = txt.at[1, pos(source), 0, :, lanes], txt.at[1, 7, 0, :, lanes]
                send(src, to, where, into, 0.5)
        return into

    def b_across(first, n):
        into, span = group(), pl.ds(first, n)
        for k in (1, 2, 3):
            send(txt.at[1, span, 0], txt.at[1, span, 4 - k], xk[k], into, n)
        return into

    scale = scale_ref[...]
    bias = bias_ref[...]

    def score(halves, gt, gi):
        first, n = halves[0], len(halves)
        texts = txt[first : first + n, 2 * gt : 2 * gt + 2].reshape(128 * n, width)
        images = img[2 * gi : 2 * gi + 2].reshape(4 * cap, width)
        raw = lax.dot_general(
            texts, images, (((1,), (1,)), ((), ())), preferred_element_type=F32
        )
        e = jnp.exp(-(scale * raw + bias))
        slope = 1.0 / (1.0 + e)
        if gt in (0, 3):
            at = 0 if gt == 0 else 64
            half_y = y // 4 if gt == 0 else 1 - y // 4
            owner = half_y * 16 + z * 2 + c
            row_ids = []
            for half in halves:
                row = lax.broadcasted_iota(jnp.int32, (128, 1), 0) - at
                named = (row >= 0) & (row < 16) & (row + BASE[half] < pairs)
                row_ids.append(jnp.where(named, owner * pairs + BASE[half] + row, -1))
            row_id = jnp.concatenate(row_ids, axis=0)
            column_id = jnp.concatenate([ids[2 * gi, 0:1], ids[2 * gi + 1, 0:1]], axis=1)
            slope = jnp.where(row_id == column_id, -e * slope, slope)
        d = (scale * slope).astype(BF16)
        for k, half in enumerate(halves):
            to = half * 512 + gt * 128
            dst[to : to + 128, gi * 256 : gi * 256 + 256] = d[128 * k : 128 * k + 128]

    def scores(tiles):
        for halves, gt, gi in tiles:
            score(halves, gt, gi)

    def known(s):
        return [(both, s, gi) for gi in range(s + 1)] + [(both, gt, s) for gt in range(s)]

    chunks = range(4)
    order = (0, 3, 1, 2)
    ax = {}
    for k in (1, 2, 3):
        ax[4 - k] = group(2)
        send(pk.at[0], pk.at[4 - k], xk[k], ax[4 - k], 1)
    bw = b_hop(1)
    waits = {}

    def start(flow, h, q):
        hop = (z_hop, a_hop)[flow]
        for side in both:
            if h <= hops_of(side, q):
                key = (flow, h, q if h < 4 else min(q, 3 - q))
                if key not in waits:
                    waits[key] = group(2 * flow)
                hop(h, side, q, waits[key])

    for q in order:
        start(0, 1, q)
    start(1, 1, 0)
    idw = group(1)
    send(id_own, id_sib, core, idw, 1)
    bx = {0: b_across(0, 1)}
    cw = {0: core_pass(0, 1)}
    for q in (3, 1, 2):
        arrive(ax[q])
        start(1, 1, q)
    arrive(idw)
    ids[0] = jnp.where(lane < cap, id_own[...], id_sib[...])
    idw = id_hop(1)
    spans = ((0, 1), (1, 2), (3, 2), (5, 2), (7, 1))
    b_spans = ((0, 1), (1, 2), (3, 2), (5, 3))

    def spread(p):
        for k in chunks:
            txt[0, p, k] = unpack(pk[4 * p + k].astype(F32)).astype(BF16)

    def forward(flow, h):
        if h < 4:
            for q in order:
                arrive(waits[flow, h, q])
                start(flow, h + 1, q)
        elif flow == 1:
            arrive(waits[flow, 4, 0], waits[flow, 4, 1])
        else:
            cw[4] = group()
            for k in both:
                arrive(waits[flow, 4, k])
                for q in (k, 3 - k):
                    rows = pl.ds(16 * q, 16)
                    send(img.at[7, 0, rows], img.at[7, 1, rows], core, cw[4], 1)
        if flow == 0 and h < 4:
            cw[h] = core_pass(*spans[h])
        elif flow == 1:
            if h == 4:
                spread(7)

    def b_forward(h):
        arrive(bw_[0])
        if h < 3:
            bw_[0] = b_hop(h + 1)
        bx[h] = b_across(*b_spans[h])

    bw_ = [bw]
    b_forward(1)
    forward(0, 1)
    arrive(idw)
    idw = id_hop(2)
    forward(1, 1)
    b_forward(2)
    forward(0, 2)
    arrive(idw)
    idw = id_hop(3)
    forward(1, 2)
    b_forward(3)
    arrive(cw[0], cw[1], bx[0], bx[1])
    for p in (0, 1):
        spread(p)
    scores(known(0))
    forward(0, 3)
    arrive(idw)
    idw = id_hop(4)
    forward(1, 3)
    arrive(cw[2], bx[2])
    for p in (2, 3):
        spread(p)
    scores(known(1))
    forward(0, 4)
    arrive(idw)
    arrive(cw[3], bx[3])
    for p in (4, 5, 6):
        spread(p)
    scores(known(2))
    scores([((1,), 3, gi) for gi in (0, 1, 2)])
    arrive(cw[4])
    scores([((1,), 3, 3)] + [(both, gt, 3) for gt in (0, 1, 2)])
    forward(1, 4)
    scores([((0,), 3, gi) for gi in (0, 1, 2, 3)])

    def image_part(gi):
        g = lax.dot_general(
            dst[:, gi * 256 : gi * 256 + 256], txt[...].reshape(1024, width),
            (((0,), (0,)), ((), ())), preferred_element_type=F32,
        ).reshape(2, 2, cap, width)
        out = [None, None]
        for k in (1, 0):
            p, out[k] = 2 * gi + k, group()
            gsend[p] = g[k, 1].astype(BF16)
            send(gsend.at[p], grecv.at[p], core, out[k], 4)
        gown[2 * gi : 2 * gi + 2] = g[:, 0]
        return out

    def text_part(gt):
        images = img[...].reshape(16 * cap, width)
        d = jnp.concatenate([dst[at : at + 128, :] for at in (gt * 128, 512 + gt * 128)], axis=0)
        t = jnp.dot(d, images, preferred_element_type=F32)
        for m in range(8):
            ta[8 * gt + m] = pack(t[16 * m : 16 * m + 16])
        t = t[128:256].reshape(2, 4, 16, width)
        tb[2 * gt : 2 * gt + 2] = t[:, 0]
        bxs[2 * gt : 2 * gt + 2] = t[:, 1:].astype(BF16)

    def text_across(gt):
        into, two = group(), pl.ds(2 * gt, 2)
        for k in (1, 2, 3):
            send(bxs.at[two, k - 1], bxr.at[two, k - 1], xk[k], into, 2)
        return into

    def image_sum(p, q):
        rows = pl.ds(16 * q, 16)
        return gown[p, rows] + grecv[p, rows].astype(F32)

    def a_sum(p, q):
        return ta[4 * p + q]

    def at(side, h, q):
        return (side * 4 + h - 1) * 4 + q

    def hop_back(flow, h, side, q):
        own, outs, ins, ends = flows[flow]
        first = 5 - hops_of(side, q)
        if h < first:
            return
        key = (flow, h, q if h > 1 else min(q, 3 - q))
        if key not in waits:
            waits[key] = group(2 * flow)
        value = own(pos((1 - 2 * side) * (5 - h)), q)
        if h > first:
            value = value + ins[at(side, h - 1, q)].astype(F32)
        spot = at(side, h, q)
        outs[spot] = value.astype(BF16)
        send(outs.at[spot], ins.at[spot], ends[side], waits[key], 1)

    def begin(flow, h):
        for q in order:
            for side in both:
                if 5 - hops_of(side, q) == h:
                    hop_back(flow, h, side, q)

    def carry(flow, h):
        for q in order:
            if h == 2:
                if q in (0, 1):
                    arrive(waits[flow, 1, q])
                hop_back(flow, 2, q // 2, q)
            else:
                arrive(waits[flow, h - 1, q])
                for side in both:
                    hop_back(flow, h, side, q)

    def ring_total(flow, q):
        own, _, ins, _ = flows[flow]
        arrive(waits[flow, 4, q])
        return own(0, q) + ins[at(0, 4, q)].astype(F32) + ins[at(1, 4, q)].astype(F32)

    def b_sum(p):
        return tb[p] + bxr[p, 0].astype(F32) + bxr[p, 1].astype(F32) + bxr[p, 2].astype(F32)

    def b_back(slot, value, where, into):
        bys[slot] = value.astype(BF16)
        send(bys.at[slot], byr.at[slot], where, into, 1)

    def b_far():
        far = group()
        b_back(0, b_sum(pos(-3)), ym, far)
        b_back(2, b_sum(pos(3)), yp, far)
        bys[1] = b_sum(pos(4)).astype(BF16)
        for where, lanes in ((ym2, left), (yp2, right)):
            send(bys.at[1, :, lanes], byr.at[1, :, lanes], where, far, 0.5)
        return far

    def came(slot):
        return byr[slot].astype(F32)

    leftish = lax.broadcasted_iota(jnp.int32, (16, width), 1) < cut
    flows = ((image_sum, zs, zr_, (zp, zm)), (a_sum, as_, ar_, (yp, ym)))
    waits = {}
    cores, across = {}, {}
    text_part(3)
    begin(1, 1)
    across[3] = text_across(3)
    cores[3] = image_part(3)
    text_part(2)
    begin(1, 2)
    across[2] = text_across(2)
    cores[2] = image_part(2)
    arrive(cores[3][1])
    begin(0, 1)
    text_part(1)
    across[1] = text_across(1)
    arrive(cores[3][0], cores[2][1])
    begin(0, 2)
    carry(1, 2)
    cores[1] = image_part(1)
    carry(0, 2)
    text_part(0)
    across[0] = text_across(0)
    carry(1, 3)
    arrive(cores[1][1], cores[2][0])
    cores[0] = image_part(0)
    carry(0, 3)
    arrive(across[3], across[2])
    far = b_far()
    carry(1, 4)
    arrive(cores[0][1], cores[1][0])
    carry(0, 4)
    arrive(across[1], across[0], far)
    near = group()
    wide = came(1)
    zeros = jnp.zeros((16, width), F32)
    b_back(3, b_sum(pos(-2)) + came(0) + jnp.where(leftish, wide, zeros), ym2, near)
    b_back(4, b_sum(pos(2)) + came(2) + jnp.where(leftish, zeros, wide), yp2, near)
    b_back(5, b_sum(pos(-1)), ym, near)
    b_back(6, b_sum(pos(1)), yp, near)
    axw = group(2)
    own_a = None
    for q in order:
        value = ring_total(1, q)
        if q == 0:
            own_a = value
        else:
            axs[q - 1] = value.astype(BF16)
            send(axs.at[q - 1], axr.at[q - 1], xk[q], axw, 1)
    arrive(cores[0][0])
    total = jnp.concatenate([ring_total(0, q) for q in chunks])
    ig_ref[...] = jnp.where(live, unit_back(total, image_unit, image_inv), 0.0)
    arrive(axw)
    total_a = own_a
    for k in range(3):
        total_a = total_a + axr[k].astype(F32)
    arrive(near)
    total_b = b_sum(0) + came(3) + came(4) + came(5) + came(6)
    total = jnp.concatenate([total_b, unpack(total_a)])[0:pairs]
    tg_ref[...] = unit_back(total, tu[0:pairs], text_inv)
    for g in outgoing:
        wait(g, False)


def hand_out(a_ref, b_ref, c_ref, d_ref):
    c_ref[...] = a_ref[...]
    d_ref[...] = b_ref[...]


def shards(tower_images, owners, counts, text, logit_scale, logit_bias):
    cap, width = tower_images.shape
    pairs = text.shape[0]
    vmem = pl.BlockSpec(memory_space=pltpu.VMEM)
    V = pltpu.VMEM
    grads = pl.pallas_call(
        kernel,
        out_shape=(
            jax.ShapeDtypeStruct((cap, width), F32),
            jax.ShapeDtypeStruct((pairs, width), F32),
        ),
        in_specs=[vmem] * 6,
        out_specs=(vmem, vmem),
        scratch_shapes=[
            V((8, 2, cap, width), BF16),
            V((8, 8, 128), jnp.int32),
            V((8, 128), jnp.int32),
            V((8, 128), jnp.int32),
            V((2, 8, 4, 16, width), BF16),
            V((32, 16, PACKED), BF16),
            V((1024, 1024), BF16),
            V((32, width), F32),
            V((8, cap, width), F32),
            V((8, cap, width), BF16),
            V((8, cap, width), BF16),
            V((32, 16, width), BF16),
            V((32, 16, width), BF16),
            V((32, 16, PACKED), F32),
            V((32, 16, PACKED), BF16),
            V((32, 16, PACKED), BF16),
            V((3, 16, PACKED), BF16),
            V((3, 16, PACKED), BF16),
            V((8, 16, width), F32),
            V((8, 3, 16, width), BF16),
            V((8, 3, 16, width), BF16),
            V((7, 16, width), BF16),
            V((7, 16, width), BF16),
            pltpu.SemaphoreType.DMA((SEMAPHORES,)),
        ],
        compiler_params=pltpu.CompilerParams(
            collective_id=0, has_side_effects=True, vmem_limit_bytes=56 << 20
        ),
    )(
        tower_images, owners.reshape(1, cap), counts.reshape(1, 1), text,
        logit_scale.reshape(1, 1), logit_bias.reshape(1, 1),
    )
    return pl.pallas_call(
        hand_out,
        out_shape=tuple(jax.ShapeDtypeStruct(g.shape, g.dtype) for g in grads),
        in_specs=[vmem, vmem],
        out_specs=(vmem, vmem),
    )(*grads)


def solution(mesh):
    split = P(("blk", "grp"))
    rows = P(("blk", "grp"), None)
    return jax.shard_map(
        shards, mesh=mesh, in_specs=(rows, split, split, rows, P(), P()), out_specs=(rows, rows),
        check_vma=False,
    )
```

```python
import jax
import jax.numpy as jnp
from jax import lax
from jax.experimental import pallas as pl
from jax.experimental.pallas import tpu as pltpu
from jax.sharding import PartitionSpec as P

MESH = pl.DeviceIdType.MESH
F32 = jnp.float32
BF16 = jnp.bfloat16
ORDER = (0, 1, -1, 2, -2, 3, -3, 4)
UNITS = 32
PACKED = 896
BASE = (16, 0)
SEMAPHORES = 112


def pos(offset):
    return ORDER.index(4 if offset == -4 else offset)


def unit_rows(values):
    wide = values.astype(F32)
    inverse = lax.rsqrt(jnp.sum(wide * wide, axis=-1, keepdims=True) + 1e-06)
    return wide * inverse, inverse


def unit_back(grad, unit, inverse):
    return (grad - unit * jnp.sum(unit * grad, axis=-1, keepdims=True)) * inverse


def pack(rows):
    low = lax.broadcasted_iota(jnp.int32, (8, 128), 0) < 4
    spare = []
    for tile in (7, 8):
        lanes = slice(128 * tile, 128 * tile + 128)
        up, down = rows[0:8, lanes], rows[8:16, lanes]
        spare += [pltpu.roll(up, 4, 0), up, pltpu.roll(down, 4, 0)]
    spare.append(jnp.zeros((8, 128), F32))
    second = [
        jnp.where(low, rows[8:16, 128 * m : 128 * m + 128], spare[m]) for m in range(7)
    ]
    return jnp.concatenate([rows[0:8, 0:PACKED], jnp.concatenate(second, axis=1)], axis=0)


def unpack(rows):
    low = lax.broadcasted_iota(jnp.int32, (8, 128), 0) < 4
    zero = jnp.zeros((8, 128), F32)
    part = [rows[8:16, 128 * m : 128 * m + 128] for m in range(7)]
    up, down = [rows[0:8]], [jnp.where(low, p, zero) for p in part]
    for m in (0, 3):
        up.append(jnp.where(low, pltpu.roll(part[m], 4, 0), part[m + 1]))
        down.append(jnp.where(low, pltpu.roll(part[m + 2], 4, 0), zero))
    return jnp.concatenate([jnp.concatenate(up, axis=1), jnp.concatenate(down, axis=1)], axis=0)


def kernel(
    img_ref, own_ref, cnt_ref, text_ref, scale_ref, bias_ref,
    ig_ref, tg_ref,
    img, ids, id_own, id_sib, txt, pk, dst, tu,
    gown, gsend, grecv, zs, zr_, ta, as_, ar_, axs, axr, tb, bxs, bxr, bys, byr,
    sems,
):
    width = img_ref.shape[1]
    cap = img_ref.shape[0]
    pairs = text_ref.shape[0]
    blk = lax.axis_index("blk")
    grp = lax.axis_index("grp")
    x, y = blk % 4, (grp // 16) * 4 + blk // 4
    z, c = (grp // 2) % 8, grp % 2

    def device(x, y, z, c):
        return ((y % 4) * 4 + x, (y // 4) * 16 + z * 2 + c)

    zp, zm = device(x, y, (z + 1) % 8, c), device(x, y, (z + 7) % 8, c)
    yp, ym = device(x, (y + 1) % 8, z, c), device(x, (y + 7) % 8, z, c)
    yp2, ym2 = device(x, (y + 2) % 8, z, c), device(x, (y + 6) % 8, z, c)
    core = device(x, y, z, 1 - c)
    xk = {k: device((x + k) % 4, y, z, c) for k in (1, 2, 3)}

    barrier = pltpu.get_barrier_semaphore()
    partners = [zp, zm, yp, ym, yp2, ym2, core, xk[1], xk[2], xk[3]]
    for p in partners:
        pl.semaphore_signal(barrier, inc=1, device_id=p, device_id_type=MESH)

    taken, outgoing = [0], []
    full = {0: zr_, 1: ids, 2: pk}

    def group(kind=0):
        taken[0] += 1
        return [taken[0] - 1, 0, kind]

    def send(src, dst_, where, into, units):
        same = [g for g in outgoing if g[2] == into[2]]
        if same and same[-1][1] + units <= UNITS:
            out = same[-1]
        else:
            out = group(into[2])
            outgoing.append(out)
        pltpu.make_async_remote_copy(
            src_ref=src, dst_ref=dst_, send_sem=sems.at[out[0]], recv_sem=sems.at[into[0]],
            device_id=where, device_id_type=MESH,
        ).start()
        out[1] += units
        into[1] += units

    def wait(done, arrived):
        whole = full[done[2]].at[pl.ds(0, int(done[1]))]
        copy = pltpu.make_async_remote_copy(
            src_ref=whole, dst_ref=whole, send_sem=sems.at[done[0]], recv_sem=sems.at[done[0]],
            device_id=core, device_id_type=MESH,
        )
        copy.wait_recv() if arrived else copy.wait_send()

    def arrive(*groups):
        for g in groups:
            wait(g, True)

    live = lax.broadcasted_iota(jnp.int32, (cap, 1), 0) < cnt_ref[...]
    image_unit, image_inv = unit_rows(img_ref[...])
    img[0, 0] = jnp.where(live, image_unit, 0.0).astype(BF16)
    lane = lax.broadcasted_iota(jnp.int32, (8, 128), 1)
    slot = jnp.where(lane < cap, lane, lane - cap)
    id_own[...] = jnp.zeros_like(id_own)
    id_own[:, 0:cap] = jnp.broadcast_to(own_ref[...], (8, cap))
    twice = jnp.where(lane < cap, id_own[...], pltpu.roll(id_own[...], cap, 1))
    id_own[...] = jnp.where(slot < cnt_ref[...], twice, -2)
    text_unit, text_inv = unit_rows(text_ref[...])
    tu[...] = jnp.zeros_like(tu)
    tu[0:pairs] = text_unit
    txt[1, 0, 0] = tu[0:16].astype(BF16)
    pk[0] = pack(tu[16:32]).astype(BF16)

    pl.semaphore_wait(barrier, len(partners))

    both = (0, 1)
    cut = 128 * ((width // 128 + 1) // 2)
    left, right = pl.ds(0, cut), pl.ds(cut, width - cut)

    def hops_of(side, q):
        return 4 if q // 2 == side else 3

    def z_hop(h, side, q, into):
        rows, sign = pl.ds(16 * q, 16), 1 - 2 * side
        send(
            img.at[pos(sign * (1 - h)), 0, rows], img.at[pos(-sign * h), 0, rows], (zp, zm)[side],
            into, 1,
        )

    def a_hop(h, side, q, into):
        sign = 1 - 2 * side
        src, to = pk.at[4 * pos(sign * (1 - h)) + q], pk.at[4 * pos(-sign * h) + q]
        send(src, to, (yp, ym)[side], into, 1)

    def id_hop(h):
        into = group(1)
        send(ids.at[pos(1 - h)], ids.at[pos(-h)], zp, into, 1)
        if h < 4:
            send(ids.at[pos(h - 1)], ids.at[pos(h)], zm, into, 1)
        return into

    def core_pass(first, n):
        into, span = group(), pl.ds(first, n)
        send(img.at[span, 0], img.at[span, 1], core, into, 4 * n)
        return into

    def b_hop(h):
        into = group()
        send(txt.at[1, pos(1 - h), 0], txt.at[1, pos(-h), 0], yp, into, 1)
        send(txt.at[1, pos(h - 1), 0], txt.at[1, pos(h), 0], ym, into, 1)
        if h == 3:
            for source, where, lanes in ((-2, yp2, left), (2, ym2, right)):
                src, to = txt.at[1, pos(source), 0, :, lanes], txt.at[1, 7, 0, :, lanes]
                send(src, to, where, into, 0.5)
        return into

    def b_across(first, n):
        into, span = group(), pl.ds(first, n)
        for k in (1, 2, 3):
            send(txt.at[1, span, 0], txt.at[1, span, 4 - k], xk[k], into, n)
        return into

    scale = scale_ref[...]
    bias = bias_ref[...]

    def score(halves, gt, gi):
        first, n = halves[0], len(halves)
        texts = txt[first : first + n, 2 * gt : 2 * gt + 2].reshape(128 * n, width)
        images = img[2 * gi : 2 * gi + 2].reshape(4 * cap, width)
        raw = lax.dot_general(
            texts, images, (((1,), (1,)), ((), ())), preferred_element_type=F32
        )
        e = jnp.exp(-(scale * raw + bias))
        slope = 1.0 / (1.0 + e)
        if gt in (0, 3):
            at = 0 if gt == 0 else 64
            half_y = y // 4 if gt == 0 else 1 - y // 4
            owner = half_y * 16 + z * 2 + c
            row_ids = []
            for half in halves:
                row = lax.broadcasted_iota(jnp.int32, (128, 1), 0) - at
                named = (row >= 0) & (row < 16) & (row + BASE[half] < pairs)
                row_ids.append(jnp.where(named, owner * pairs + BASE[half] + row, -1))
            row_id = jnp.concatenate(row_ids, axis=0)
            column_id = jnp.concatenate([ids[2 * gi, 0:1], ids[2 * gi + 1, 0:1]], axis=1)
            slope = jnp.where(row_id == column_id, -e * slope, slope)
        d = (scale * slope).astype(BF16)
        for k, half in enumerate(halves):
            to = half * 512 + gt * 128
            dst[to : to + 128, gi * 256 : gi * 256 + 256] = d[128 * k : 128 * k + 128]

    def scores(tiles):
        for halves, gt, gi in tiles:
            score(halves, gt, gi)

    def known(s):
        return [(both, s, gi) for gi in range(s + 1)] + [(both, gt, s) for gt in range(s)]

    chunks = range(4)
    order = (0, 3, 1, 2)
    ax = {}
    for k in (1, 2, 3):
        ax[4 - k] = group(2)
        send(pk.at[0], pk.at[4 - k], xk[k], ax[4 - k], 1)
    bw = b_hop(1)
    waits = {}

    def start(flow, h, q):
        hop = (z_hop, a_hop)[flow]
        for side in both:
            if h <= hops_of(side, q):
                key = (flow, h, q if h < 4 else min(q, 3 - q))
                if key not in waits:
                    waits[key] = group(2 * flow)
                hop(h, side, q, waits[key])

    for q in order:
        start(0, 1, q)
    start(1, 1, 0)
    idw = group(1)
    send(id_own, id_sib, core, idw, 1)
    bx = {0: b_across(0, 1)}
    cw = {0: core_pass(0, 1)}
    for q in (3, 1, 2):
        arrive(ax[q])
        start(1, 1, q)
    arrive(idw)
    ids[0] = jnp.where(lane < cap, id_own[...], id_sib[...])
    idw = id_hop(1)
    spans = ((0, 1), (1, 2), (3, 2), (5, 2), (7, 1))
    b_spans = ((0, 1), (1, 2), (3, 2), (5, 3))

    def spread(p):
        for k in chunks:
            txt[0, p, k] = unpack(pk[4 * p + k].astype(F32)).astype(BF16)

    def forward(flow, h):
        if h < 4:
            for q in order:
                arrive(waits[flow, h, q])
                start(flow, h + 1, q)
        elif flow == 1:
            arrive(waits[flow, 4, 0], waits[flow, 4, 1])
        else:
            cw[4] = group()
            for k in both:
                arrive(waits[flow, 4, k])
                for q in (k, 3 - k):
                    rows = pl.ds(16 * q, 16)
                    send(img.at[7, 0, rows], img.at[7, 1, rows], core, cw[4], 1)
        if flow == 0 and h < 4:
            cw[h] = core_pass(*spans[h])
        elif flow == 1:
            if h == 4:
                spread(7)

    def b_forward(h):
        arrive(bw_[0])
        if h < 3:
            bw_[0] = b_hop(h + 1)
        bx[h] = b_across(*b_spans[h])

    bw_ = [bw]
    b_forward(1)
    forward(0, 1)
    arrive(idw)
    idw = id_hop(2)
    forward(1, 1)
    b_forward(2)
    forward(0, 2)
    arrive(idw)
    idw = id_hop(3)
    forward(1, 2)
    b_forward(3)
    arrive(cw[0], cw[1], bx[0], bx[1])
    for p in (0, 1):
        spread(p)
    scores(known(0))
    forward(0, 3)
    arrive(idw)
    idw = id_hop(4)
    forward(1, 3)
    arrive(cw[2], bx[2])
    for p in (2, 3):
        spread(p)
    scores(known(1))
    forward(0, 4)
    arrive(idw)
    arrive(cw[3], bx[3])
    for p in (4, 5, 6):
        spread(p)
    scores(known(2))
    scores([((1,), 3, gi) for gi in (0, 1, 2)])
    arrive(cw[4])
    scores([((1,), 3, 3)] + [(both, gt, 3) for gt in (0, 1, 2)])
    forward(1, 4)
    scores([((0,), 3, gi) for gi in (0, 1, 2, 3)])

    def image_part(gi):
        g = lax.dot_general(
            dst[:, gi * 256 : gi * 256 + 256], txt[...].reshape(1024, width),
            (((0,), (0,)), ((), ())), preferred_element_type=F32,
        ).reshape(2, 2, cap, width)
        out = [None, None]
        for k in (1, 0):
            p, out[k] = 2 * gi + k, group()
            gsend[p] = g[k, 1].astype(BF16)
            send(gsend.at[p], grecv.at[p], core, out[k], 4)
        gown[2 * gi : 2 * gi + 2] = g[:, 0]
        return out

    def text_part(gt):
        images = img[...].reshape(16 * cap, width)
        d = jnp.concatenate([dst[at : at + 128, :] for at in (gt * 128, 512 + gt * 128)], axis=0)
        t = jnp.dot(d, images, preferred_element_type=F32)
        for m in range(8):
            ta[8 * gt + m] = pack(t[16 * m : 16 * m + 16])
        t = t[128:256].reshape(2, 4, 16, width)
        tb[2 * gt : 2 * gt + 2] = t[:, 0]
        bxs[2 * gt : 2 * gt + 2] = t[:, 1:].astype(BF16)

    def text_across(gt):
        into, two = group(), pl.ds(2 * gt, 2)
        for k in (1, 2, 3):
            send(bxs.at[two, k - 1], bxr.at[two, k - 1], xk[k], into, 2)
        return into

    def image_sum(p, q):
        rows = pl.ds(16 * q, 16)
        return gown[p, rows] + grecv[p, rows].astype(F32)

    def a_sum(p, q):
        return ta[4 * p + q]

    def at(side, h, q):
        return (side * 4 + h - 1) * 4 + q

    def hop_back(flow, h, side, q):
        own, outs, ins, ends = flows[flow]
        first = 5 - hops_of(side, q)
        if h < first:
            return
        key = (flow, h, q if h > 1 else min(q, 3 - q))
        if key not in waits:
            waits[key] = group(2 * flow)
        value = own(pos((1 - 2 * side) * (5 - h)), q)
        if h > first:
            value = value + ins[at(side, h - 1, q)].astype(F32)
        spot = at(side, h, q)
        outs[spot] = value.astype(BF16)
        send(outs.at[spot], ins.at[spot], ends[side], waits[key], 1)

    def begin(flow, h):
        for q in order:
            for side in both:
                if 5 - hops_of(side, q) == h:
                    hop_back(flow, h, side, q)

    def carry(flow, h):
        for q in order:
            if h == 2:
                if q in (0, 1):
                    arrive(waits[flow, 1, q])
                hop_back(flow, 2, q // 2, q)
            else:
                arrive(waits[flow, h - 1, q])
                for side in both:
                    hop_back(flow, h, side, q)

    def ring_total(flow, q):
        own, _, ins, _ = flows[flow]
        arrive(waits[flow, 4, q])
        return own(0, q) + ins[at(0, 4, q)].astype(F32) + ins[at(1, 4, q)].astype(F32)

    def b_sum(p):
        return tb[p] + bxr[p, 0].astype(F32) + bxr[p, 1].astype(F32) + bxr[p, 2].astype(F32)

    def b_back(slot, value, where, into):
        bys[slot] = value.astype(BF16)
        send(bys.at[slot], byr.at[slot], where, into, 1)

    def b_far():
        far = group()
        b_back(0, b_sum(pos(-3)), ym, far)
        b_back(2, b_sum(pos(3)), yp, far)
        bys[1] = b_sum(pos(4)).astype(BF16)
        for where, lanes in ((ym2, left), (yp2, right)):
            send(bys.at[1, :, lanes], byr.at[1, :, lanes], where, far, 0.5)
        return far

    def came(slot):
        return byr[slot].astype(F32)

    leftish = lax.broadcasted_iota(jnp.int32, (16, width), 1) < cut
    flows = ((image_sum, zs, zr_, (zp, zm)), (a_sum, as_, ar_, (yp, ym)))
    waits = {}
    cores, across = {}, {}
    text_part(3)
    begin(1, 1)
    across[3] = text_across(3)
    cores[3] = image_part(3)
    text_part(2)
    begin(1, 2)
    across[2] = text_across(2)
    cores[2] = image_part(2)
    arrive(cores[3][1])
    begin(0, 1)
    text_part(1)
    across[1] = text_across(1)
    arrive(cores[3][0], cores[2][1])
    begin(0, 2)
    carry(1, 2)
    cores[1] = image_part(1)
    carry(0, 2)
    text_part(0)
    across[0] = text_across(0)
    carry(1, 3)
    arrive(cores[1][1], cores[2][0])
    cores[0] = image_part(0)
    carry(0, 3)
    arrive(across[3], across[2])
    far = b_far()
    carry(1, 4)
    arrive(cores[0][1], cores[1][0])
    carry(0, 4)
    axw = group(2)
    own_a = None
    for q in order:
        value = ring_total(1, q)
        if q == 0:
            own_a = value
        else:
            axs[q - 1] = value.astype(BF16)
            send(axs.at[q - 1], axr.at[q - 1], xk[q], axw, 1)
    arrive(cores[0][0])
    arrive(across[1], across[0], far)
    near = group()
    wide = came(1)
    zeros = jnp.zeros((16, width), F32)
    b_back(3, b_sum(pos(-2)) + came(0) + jnp.where(leftish, wide, zeros), ym2, near)
    b_back(4, b_sum(pos(2)) + came(2) + jnp.where(leftish, zeros, wide), yp2, near)
    b_back(5, b_sum(pos(-1)), ym, near)
    b_back(6, b_sum(pos(1)), yp, near)
    total = jnp.concatenate([ring_total(0, q) for q in chunks])
    ig_ref[...] = jnp.where(live, unit_back(total, image_unit, image_inv), 0.0)
    arrive(axw)
    total_a = own_a
    for k in range(3):
        total_a = total_a + axr[k].astype(F32)
    arrive(near)
    total_b = b_sum(0) + came(3) + came(4) + came(5) + came(6)
    total = jnp.concatenate([total_b, unpack(total_a)])[0:pairs]
    tg_ref[...] = unit_back(total, tu[0:pairs], text_inv)
    for g in outgoing:
        wait(g, False)


def hand_out(a_ref, b_ref, c_ref, d_ref, a_held, b_held, sems):
    pieces = [(b_ref, b_held, d_ref)]
    for first in range(0, a_ref.shape[0], 16):
        rows = pl.ds(first, 16)
        pieces.append((a_ref.at[rows], a_held.at[rows], c_ref.at[rows]))
    into = [
        pltpu.make_async_copy(src, held, sems.at[0, k]) for k, (src, held, _) in enumerate(pieces)
    ]
    out = [
        pltpu.make_async_copy(held, to, sems.at[1, k]) for k, (_, held, to) in enumerate(pieces)
    ]
    for copy in into:
        copy.start()
    for arriving, leaving in zip(into, out):
        arriving.wait()
        leaving.start()
    for copy in out:
        copy.wait()


def shards(tower_images, owners, counts, text, logit_scale, logit_bias):
    cap, width = tower_images.shape
    pairs = text.shape[0]
    vmem = pl.BlockSpec(memory_space=pltpu.VMEM)
    V = pltpu.VMEM
    grads = pl.pallas_call(
        kernel,
        out_shape=(
            jax.ShapeDtypeStruct((cap, width), F32),
            jax.ShapeDtypeStruct((pairs, width), F32),
        ),
        in_specs=[vmem] * 6,
        out_specs=(vmem, vmem),
        scratch_shapes=[
            V((8, 2, cap, width), BF16),
            V((8, 8, 128), jnp.int32),
            V((8, 128), jnp.int32),
            V((8, 128), jnp.int32),
            V((2, 8, 4, 16, width), BF16),
            V((32, 16, PACKED), BF16),
            V((1024, 1024), BF16),
            V((32, width), F32),
            V((8, cap, width), F32),
            V((8, cap, width), BF16),
            V((8, cap, width), BF16),
            V((32, 16, width), BF16),
            V((32, 16, width), BF16),
            V((32, 16, PACKED), F32),
            V((32, 16, PACKED), BF16),
            V((32, 16, PACKED), BF16),
            V((3, 16, PACKED), BF16),
            V((3, 16, PACKED), BF16),
            V((8, 16, width), F32),
            V((8, 3, 16, width), BF16),
            V((8, 3, 16, width), BF16),
            V((7, 16, width), BF16),
            V((7, 16, width), BF16),
            pltpu.SemaphoreType.DMA((SEMAPHORES,)),
        ],
        compiler_params=pltpu.CompilerParams(
            collective_id=0, has_side_effects=True, vmem_limit_bytes=56 << 20
        ),
    )(
        tower_images, owners.reshape(1, cap), counts.reshape(1, 1), text,
        logit_scale.reshape(1, 1), logit_bias.reshape(1, 1),
    )
    anywhere = pl.BlockSpec(memory_space=pl.ANY)
    return pl.pallas_call(
        hand_out,
        out_shape=tuple(jax.ShapeDtypeStruct(g.shape, g.dtype) for g in grads),
        in_specs=[anywhere, anywhere],
        out_specs=(anywhere, anywhere),
        scratch_shapes=[
            V((cap, width), F32), V((pairs, width), F32),
            pltpu.SemaphoreType.DMA((2, 1 + cap // 16)),
        ],
    )(*grads)


def solution(mesh):
    split = P(("blk", "grp"))
    rows = P(("blk", "grp"), None)
    return jax.shard_map(
        shards, mesh=mesh, in_specs=(rows, split, split, rows, P(), P()), out_specs=(rows, rows),
        check_vma=False,
    )
```
